256 devices in a mesh: section: 4 (over x_lo, core), peer: 64 (over z, y, x_hi).
Axes of the slice: x: 4 (x_hi: 2, x_lo: 2; x = x_hi * 2 + x_lo), y: 4, z: 8, core: 2. Of those that a mesh axis runs over, the one named last changes fastest.
Arguments:
- send_grads: bfloat16 [32768, 5120], P(('section', 'peer')), may hold values from -6 to 6
- wiring: int32 [32768, 1], P(('section', 'peer')), may hold values from 0 to 63; in each aligned block of 128 rows (0 to 127, 128 to 255, ...) at most 4 rows name the same one
- loss_grad: bfloat16 [16384, 5120], P('peer'), may hold values from -6 to 6
- saved_acts: bfloat16 [65536, 5120], P(('section', 'peer')), may hold values from -6 to 6
- gain: float32 [4, 5120], P('section'), may hold values from 0.1 to 1.9
- lagged_grads: bfloat16 [256, 327680], P('section', 'peer'), may hold values from -16 to 16
- weights: float32 [256, 5120], P('section'), may hold values from -6 to 6
Outputs:
- input_grads: bfloat16 [65536, 5120], P(('section', 'peer'))
- new_weights: float32 [256, 5120], P('section')
The draws below stay inside these ranges and needn't reach their ends.
Inputs may be any that keep to these rules, and one draw needn't show every extreme that they name: `wiring`: among the rows of one device, at most 4 name the same peer; some peer is named exactly 4 times.
All inputs are finite; a program needn't handle non-finite values.
Results may differ from the reference program's by a relative error of at most 0.001.
Values may be sent and summed in bfloat16 or wider, within the bound.
A program may use at most 64 MiB of HBM per device.

```python
import math
import jax
import jax.numpy as jnp
import numpy as np
from jax import lax

D = 5120
ROWS_DEV = 128
GRAD_ROWS = 64
CAP = 4
SLOTS = 256
N_SECTION = 4
N_PEER = 64


def spiked(result, stream_key, source, target, parts, factor):
    def block_of(axis_at):
        return (jnp.arange(result.shape[axis_at]) // (result.shape[axis_at] // parts)).reshape((-1,) + (1,) * (result.ndim - 1 - axis_at))

    one_side = jax.random.permutation(stream_key, parts)[block_of(target)]
    far = (block_of(target) + parts // 2) % parts
    return jnp.where((block_of(source) == one_side) | (block_of(source) == far), factor * result, result)


def level_of(own_key, dims, split, smallest, high):
    loudness, own = 1.0, jax.random.fold_in(own_key, 6)
    for axis_at, parts in split:
        heights = jnp.exp(jax.random.uniform(jax.random.fold_in(own, axis_at), (parts,), jnp.float32, smallest / len(split), high / len(split)))
        loudness = loudness * jnp.repeat(heights, dims[axis_at] // parts).reshape([-1 if axis == axis_at else 1 for axis in range(len(dims))])
    return loudness


def shared_out(rng, own, number, rows, count, top, bound, lean):
    ranking = jax.random.permutation(rng, count)
    heavy_load, common = shares(count, rows * top, bound, lean, True), shares(count, rows * top, bound, lean, False)
    places = jnp.arange(count)

    def named(lengths, turn):
        used = int((lengths > 0).sum())
        fixed = max(1, used // 4)
        moved = fixed + (places - fixed + turn * (used - fixed)) % max(1, count - fixed)
        return jnp.zeros((count,), jnp.int32).at[ranking[jnp.where(places < fixed, places, moved)]].set(jnp.asarray(lengths, jnp.int32))

    lengths = jnp.where(number % 4 == 0, named(heavy_load, number // 4), named(common, number - number // 4 - 1))
    mixed = jax.random.permutation(jax.random.fold_in(own, 3), count)
    giver, taker = mixed[0:count // 2 * 2:2], mixed[1:count // 2 * 2:2]
    room = jnp.minimum(lengths[giver] - 1, bound - lengths[taker]) // 2
    room = jnp.where((giver == ranking[0]) | (taker == ranking[0]) | (lengths[taker] == 0), 0, jnp.maximum(room, 0))
    moved = jax.random.randint(jax.random.fold_in(own, 4), (count // 2,), 0, 1 << 20) % (room + 1)
    lengths = lengths.at[giver].add(-moved).at[taker].add(moved)
    members = jnp.searchsorted(jnp.cumsum(lengths), jnp.arange(rows * top), side="right").astype(jnp.int32)
    table = members.reshape(top, rows).T
    table = table[jax.random.permutation(jax.random.fold_in(own, 1), rows)]
    turn = jax.random.randint(jax.random.fold_in(own, 2), (rows, 1), 0, top)
    return jnp.take_along_axis(table, (jnp.arange(top)[None, :] + turn) % top, axis=1)


def shares(number_of, total, most, slope, full):
    portions = [(1 << 20) // math.isqrt(standing ** slope) + 1 for standing in range(1, number_of + 1)]
    largest = most if full else min(most, max(-(-total // number_of), total * portions[0] // sum(portions)))
    least = 1 if total - largest >= number_of - 1 else 0
    holding, rest = [largest] + [least] * (number_of - 1), total - largest - least * (number_of - 1)
    while rest > 0:
        movable = [i for i in range(1, number_of) if holding[i] < largest] or [i for i in range(1, number_of) if holding[i] < most]
        pool, left = sum([portions[i] for i in movable]), rest
        for i in movable:
            extra = min(most - holding[i], max(1, left * portions[i] // pool), rest)
            holding[i] = holding[i] + extra
            rest = rest - extra
    return np.array(holding)


def scatter_about(key, extent, deviation, limit, shards=(), kind=jnp.bfloat16):
    values = jax.random.normal(key, extent, jnp.float32) * deviation
    if len(shards) > 0:
        values = level_of(key, extent, shards, -0.22, 0.18) * values
    return jnp.clip(values, min=-limit, max=limit).astype(kind)


def bell_draw_with(stream_key, extent, spread, reach, pieces, heavy, held_as=jnp.bfloat16):
    result = spread * jax.random.normal(stream_key, extent, jnp.float32)
    if pieces:
        result = result * level_of(stream_key, extent, pieces, -0.22, 0.18)
    return jnp.clip(spiked(result, jax.random.fold_in(stream_key, 3), *heavy), -reach, reach).astype(held_as)


def setup_inputs(seed: int = 0) -> dict:
    streams_of = jax.random.split(jax.random.key(seed), 8)
    send_grads = scatter_about(streams_of[0], (N_SECTION * N_PEER * ROWS_DEV, D), 1.0, 6.0, ((0, 256),))
    wiring_keys = jax.random.split(jax.random.fold_in(streams_of[1], 1), (N_SECTION * N_PEER * ROWS_DEV) // ROWS_DEV)
    wiring_turns = jax.random.permutation(jax.random.fold_in(streams_of[1], 3), (N_SECTION * N_PEER * ROWS_DEV) // ROWS_DEV)
    wiring = jax.vmap(lambda own, number: shared_out(jax.random.fold_in(streams_of[1], 2), own, number, ROWS_DEV, N_PEER, 1, CAP, 2))(wiring_keys, wiring_turns).reshape((N_SECTION * N_PEER * ROWS_DEV, 1))
    loss_grad = scatter_about(streams_of[2], (N_PEER * SLOTS, D), 1.0, 6.0, ((0, 64),))
    saved_acts = scatter_about(streams_of[3], (N_SECTION * N_PEER * SLOTS, D), 1.0, 6.0, ((0, 256),))
    gain = jnp.clip(1.0 + 0.18 * jax.random.normal(streams_of[4], (N_SECTION, D), jnp.float32), 0.1, 1.9)
    lagged_grads = bell_draw_with(streams_of[5], (N_SECTION * GRAD_ROWS, N_PEER * D), 1.0, 16.0, ((0, 4), (1, 64)), (1, 0, 64, 4.0))
    weights = scatter_about(streams_of[6], (N_SECTION * GRAD_ROWS, D), 1.0, 6.0, ((0, 4),), jnp.float32)
    return dict(send_grads=send_grads, wiring=wiring, loss_grad=loss_grad, saved_acts=saved_acts, gain=gain, lagged_grads=lagged_grads, weights=weights)


def arrange(rows, wires):
    dest = wires[:, 0]
    onehot = (dest[:, None] == jnp.arange(N_PEER, dtype=jnp.int32)[None, :]).astype(jnp.int32)
    before = jnp.cumsum(onehot, axis=0) - onehot
    rank = lax.optimization_barrier(jnp.sum(before * onehot, axis=1))
    index = (dest * CAP + rank).astype(jnp.int32)
    empty = jnp.zeros((N_PEER * CAP, rows.shape[1]), rows.dtype)
    return empty.at[index].set(rows)

def norm_back(grads, acts, gains):
    g = grads.astype(jnp.float32)
    x = acts.astype(jnp.float32)
    scale = lax.rsqrt(lax.optimization_barrier(jnp.mean(x * x, axis=-1, keepdims=True)) + 1e-05)
    normed = x * scale
    dy = g * gains[None, :]
    inner = lax.optimization_barrier(jnp.mean(dy * normed, axis=-1, keepdims=True))
    return (g + (dy - normed * inner) * scale).astype(jnp.bfloat16)

def reference(send_grads, wiring, loss_grad, saved_acts, gain, lagged_grads, weights):
    sends = send_grads.reshape(N_SECTION, N_PEER, ROWS_DEV, D)
    wires = wiring.reshape(N_SECTION, N_PEER, ROWS_DEV, 1)
    saved = saved_acts.reshape(N_SECTION, N_PEER, SLOTS, D)
    loss_slots = loss_grad.reshape(N_PEER, SLOTS, D)

    def one_section(section_id):
        upper = jnp.minimum(section_id + 1, N_SECTION - 1)
        bufs = jax.vmap(arrange)(sends[upper], wires[upper])
        bufs = bufs.reshape(N_PEER, N_PEER, CAP, D)
        arrived = jnp.transpose(bufs, (1, 0, 2, 3)).reshape(N_PEER, SLOTS, D)
        incoming = jnp.where(section_id == N_SECTION - 1, loss_slots, arrived)
        gains = gain[section_id]
        return jax.vmap(lambda g, x: norm_back(g, x, gains))(incoming, saved[section_id])
    outs = lax.map(one_section, jnp.arange(N_SECTION, dtype=jnp.int32))
    input_grads = outs.reshape(N_SECTION * N_PEER * SLOTS, D)
    grads = lagged_grads.astype(jnp.float32).reshape(N_SECTION * GRAD_ROWS, N_PEER, D)
    mean_grad = lax.optimization_barrier(jnp.sum(grads, axis=1)) / N_PEER
    new_weights = weights - 0.5 * mean_grad
    return (input_grads, new_weights)
```

```python
import functools

import jax
import jax.numpy as jnp
from jax import lax
from jax.experimental import pallas as pl
from jax.experimental.pallas import tpu as pltpu
from jax.sharding import PartitionSpec as P

MESH = pl.DeviceIdType.MESH
SLOTS = 256
CAP = 4
PIECES = 8
AHEAD = 8


def place():
    s = lax.axis_index("section")
    p = lax.axis_index("peer")
    return s, p // 8, (p // 2) % 4, p % 2


def iota(shape, dim):
    return lax.broadcasted_iota(jnp.int32, shape, dim)


def slot_matrix(wire, z, y, h):
    rows = wire.shape[1]
    r, c = iota((rows, rows), 0), iota((rows, rows), 1)
    across = jnp.broadcast_to(wire, (rows, rows))
    down = jnp.sum(jnp.where(r == c, across, 0), axis=1, keepdims=True)
    rank = jnp.sum(jnp.where((down == across) & (r < c), 1, 0), axis=0, keepdims=True)
    key = wire * CAP + rank
    i = iota((SLOTS, rows), 0)
    dh, d, dy, k = i >> 7, (i >> 4) & 7, (i >> 2) & 3, i & 3
    q = ((z + d) & 7) * 8 + ((y + dy) & 3) * 2 + ((h + dh) & 1)
    return jnp.where(q * CAP + k == key, 1.0, 0.0).astype(jnp.bfloat16)


def regroup_matrix():
    o, i = iota((SLOTS, SLOTS), 0), iota((SLOTS, SLOTS), 1)
    dy, dh, d, k = o >> 6, (o >> 5) & 1, (o >> 2) & 7, o & 3
    return jnp.where(dh * 128 + d * 16 + dy * 4 + k == i, 1.0, 0.0).astype(jnp.bfloat16)


def natural_matrix(z, y, h):
    n, o = iota((SLOTS, SLOTS), 0), iota((SLOTS, SLOTS), 1)
    zs, ys, hs, k = n >> 5, (n >> 3) & 3, (n >> 2) & 1, n & 3
    d, dy, dh = (z - zs) & 7, (y - ys) & 3, (h - hs) & 1
    return jnp.where((dy * 2 + dh) * 32 + d * 4 + k == o, 1.0, 0.0).astype(jnp.bfloat16)


def exchange(pieces, cols, wire, rows_ref, lag_ref, w_ref, arrived, new_w,
             send1, recv1, send2, slots, regroup, lag_in, part, part_in, fresh,
             s0, r0, s1, r1, s2, r2, sa, ra, local):
    s, z, y, h = place()
    width = lag_ref.shape[1]
    block = width // 8

    def at(section, dz, dy, dh):
        peer = ((z + dz) % 8) * 8 + ((y + dy) % 4) * 2 + (h + dh) % 2
        return (section, peer)

    def push(src, dst, ssem, rsem, to):
        return pltpu.make_async_remote_copy(src_ref=src, dst_ref=dst, send_sem=ssem, recv_sem=rsem,
                                            device_id=to, device_id_type=MESH)

    me = at(s, 0, 0, 0)
    barrier = pltpu.get_barrier_semaphore()
    for d in range(1, 8):
        pl.semaphore_signal(barrier, inc=1, device_id=at(s, d, 0, 0), device_id_type=MESH)
    for e in range(8):
        for ds in range(4):
            if e or ds:
                pl.semaphore_signal(barrier, inc=1, device_id=at((s + ds) % 4, 0, e // 2, e % 2), device_id_type=MESH)

    sends = s >= 1
    crossing = lambda i: lax.rem(i, 2) == 1

    slots[...] = slot_matrix(wire[...], z, y, h)
    regroup[...] = regroup_matrix()

    def span(i):
        return pl.ds(pl.multiple_of(i * cols, 128), cols)

    def arrange(i, carry):
        out = jnp.dot(slots[...], rows_ref[:, span(i)], preferred_element_type=jnp.float32).astype(jnp.bfloat16)
        out = out.reshape(2, 128, cols)
        send1[i] = out
        recv1[i, :, 0:16, :] = out[:, 0:16, :]
        return carry

    @pl.when((s == 1) | (s == 3))
    def _():
        lax.fori_loop(0, pieces, arrange, 0)

    @pl.when(s == 2)
    def _():
        lax.fori_loop(0, pieces, arrange, 0)

    pl.semaphore_wait(barrier, 38)

    def lag_copy(e):
        dy, dh = e // 2, e % 2
        j = ((y + dy) % 4) * 2 + (h + dh) % 2
        return push(lag_ref.at[:, pl.ds(pl.multiple_of(j * block, 128), block)], lag_in.at[e - 1], sa.at[0], ra.at[0],
                    at(s, 0, dy, dh))

    for e in range(1, 8):
        lag_copy(e).start()

    def along_z(i, d):
        lines = pl.ds(d * 16, 16)
        return push(send1.at[i, :, lines, :], recv1.at[i, :, lines, :], s1.at[i], r1.at[i], at(s, d, 0, 0))

    def along_z_all(i):
        lines = pl.ds(16, 112)
        return push(send1.at[i, :, lines, :], recv1.at[i, :, lines, :], s1.at[i], r1.at[i], at(s, 1, 0, 0))

    def start_z(i):
        for d in (4, 3, 5, 2, 6, 1, 7):
            along_z(i, d).start()

    def cross(i, dh, first):
        lines = pl.ds(0, 16) if first else pl.ds(16, 112)
        return push(send1.at[i, dh, lines, :], (recv1 if first else send1).at[i, dh, lines, :],
                    s0.at[i], r0.at[i], at(0, 0, 0, dh))

    def whole(buffer, i, ssem, rsem):
        return push(buffer.at[i], buffer.at[i], ssem.at[i], rsem.at[i], at((s + 3) % 4, 0, 0, 0))

    def start_out(i, carry):
        @pl.when((s == 1) | (s == 3) | ((s == 2) & ~crossing(i)))
        def _():
            start_z(i)

        @pl.when((s == 2) & crossing(i))
        def _():
            for dh in range(2):
                cross(i, dh, False).start()
                cross(i, dh, True).start()

        return carry

    lax.fori_loop(0, pieces, start_out, 0)

    @pl.when(s == 0)
    def _():
        def onward(i, carry):
            @pl.when(crossing(i))
            def _():
                whole(send2, i, s0, r0).wait_recv()
                start_z(i)
            return carry
        lax.fori_loop(0, pieces, onward, 0)

    mine = (y * 2 + h) * block
    own = pl.ds(pl.multiple_of(mine, 128), block)
    zrows = pl.ds(pl.multiple_of(z * 8, 8), 8)

    def lag_sum():
        push(lag_in, lag_in, sa.at[0], ra.at[0], me).wait_recv()
        total = lag_ref[:, own].astype(jnp.float32)
        for e in range(7):
            total = total + lag_in[e].astype(jnp.float32)
        part[...] = total
        for d in range(1, 8):
            to = (z + d) % 8
            push(part.at[pl.ds(pl.multiple_of(to * 8, 8), 8)], part_in.at[d - 1], sa.at[1], ra.at[1],
                 at(s, d, 0, 0)).start()

    def update():
        push(part_in, part_in, sa.at[1], ra.at[1], me).wait_recv()
        total = part[zrows, :]
        for d in range(7):
            total = total + part_in[d]
        fresh[...] = w_ref[zrows, own] - 0.5 * (total / 64.0)
        for d in range(1, 8):
            push(fresh, new_w.at[zrows, own], sa.at[2], ra.at[2], at(s, d, 0, 0)).start()
        pltpu.make_async_copy(fresh, new_w.at[zrows, own], local).start()

    def gather_h():
        push(part_in, part_in, sa.at[2], ra.at[2], me).wait_recv()
        pltpu.make_async_copy(fresh, new_w.at[zrows, own], local).wait()
        push(new_w.at[:, own], new_w.at[:, own], sa.at[3], ra.at[3], at(s, 0, 0, 1)).start()

    pair = pl.ds(pl.multiple_of(y * 2 * block, 128), 2 * block)

    def gather_y():
        push(part, part, sa.at[3], ra.at[3], me).wait_recv()
        for dy in (2, 1, 3):
            push(new_w.at[:, pair], new_w.at[:, pair], sa.at[4], ra.at[4], at(s, 0, dy, 0)).start()

    three = pl.ds(0, 6 * block)

    def relay(i):
        along_z_all(i).wait_recv()
        data = recv1[i].reshape(SLOTS, cols)
        send2[i] = jnp.dot(regroup[...], data, preferred_element_type=jnp.float32).astype(jnp.bfloat16)

        @pl.when(s >= 1)
        def _():
            for e in (4, 5, 2, 3, 6, 7, 1, 0):
                lines = pl.ds(e * 32, 32)
                push(send2.at[i, lines, :], arrived.at[i, lines, :], s2.at[i], r2.at[i],
                     at((s + 3) % 4, 0, e // 2, e % 2)).start()

        @pl.when(s == 0)
        def _():
            for dy in (2, 1, 3, 0):
                lines = pl.ds(dy * 64, 64)
                push(send2.at[i, lines, :], arrived.at[i, lines, :], s2.at[i], r2.at[i], at(1, 0, dy, 0)).start()

    relays = lambda i: (s == 1) | (s == 3) | ((s == 2) & ~crossing(i)) | ((s == 0) & crossing(i))

    def step(i, carry):
        pl.when(i == 0)(lag_sum)
        pl.when(i == 1)(update)
        pl.when(i == 2)(gather_h)
        pl.when(i == 3)(gather_y)
        pl.when(relays(i))(lambda: relay(i))
        return carry

    lax.fori_loop(0, pieces, step, 0)

    def finish(i, carry):
        @pl.when(relays(i))
        def _():
            along_z_all(i).wait_send()
            whole(send2, i, s2, r2).wait_send()

        @pl.when((s == 2) & crossing(i))
        def _():
            whole(send2, i, s0, r0).wait_send()

        @pl.when(s <= 2)
        def _():
            whole(arrived, i, s2, r2).wait_recv()

        return carry

    lax.fori_loop(0, pieces, finish, 0)
    push(lag_in, lag_in, sa.at[0], ra.at[0], me).wait_send()
    push(part_in, part_in, sa.at[1], ra.at[1], me).wait_send()
    push(part_in, part_in, sa.at[2], ra.at[2], me).wait_send()
    push(part, part, sa.at[3], ra.at[3], me).wait_send()
    push(new_w.at[:, three], new_w.at[:, three], sa.at[4], ra.at[4], me).wait()


def norm(pieces, cols, arrived, loss, acts, gain, out, grads, natural):
    s, z, y, h = place()
    width = acts.shape[1]
    natural[...] = natural_matrix(z, y, h)

    def span(i):
        return pl.ds(pl.multiple_of(i * cols, 128), cols)

    @pl.when(s == 3)
    def _():
        grads[...] = loss[...]

    def bring(i, carry):
        @pl.when(s < 3)
        def _():
            grads[:, span(i)] = jnp.dot(natural[...], arrived[i], preferred_element_type=jnp.float32).astype(jnp.bfloat16)
        return carry

    lax.fori_loop(0, pieces, bring, 0)

    def lines(b, carry):
        rows = pl.ds(pl.multiple_of(b * 16, 16), 16)

        def sums(i, both):
            x = acts[rows, span(i)].astype(jnp.float32)
            g = grads[rows, span(i)].astype(jnp.float32)
            a = jnp.sum(x * x, axis=1, keepdims=True)
            c = jnp.sum(g * gain[:, span(i)] * x, axis=1, keepdims=True)
            return both[0] + a, both[1] + c

        zero = jnp.zeros((16, 1), jnp.float32)
        a, c = lax.fori_loop(0, pieces, sums, (zero, zero), unroll=True)
        r = lax.rsqrt(a / width + 1e-05)
        inner = c * r / width

        def last(i, carry):
            x = acts[rows, span(i)].astype(jnp.float32)
            g = grads[rows, span(i)].astype(jnp.float32)
            out[rows, span(i)] = (g + (g * gain[:, span(i)] - (x * r) * inner) * r).astype(jnp.bfloat16)
            return carry

        lax.fori_loop(0, pieces, last, 0, unroll=True)
        return carry

    lax.fori_loop(0, SLOTS // 16, lines, 0)


def per_device(send_grads, wiring, loss_grad, saved_acts, gain, lagged_grads, weights):
    rows, width = send_grads.shape
    pieces, cols = PIECES, width // PIECES
    depth = lagged_grads.shape[0]
    block = width // 8
    vmem = pl.BlockSpec(memory_space=pltpu.VMEM)
    hbm = pl.BlockSpec(memory_space=pl.ANY)
    bf16, f32 = jnp.bfloat16, jnp.float32
    dma = pltpu.SemaphoreType.DMA
    arrived, new_weights = pl.pallas_call(
        functools.partial(exchange, pieces, cols),
        out_shape=(
            jax.ShapeDtypeStruct((pieces, SLOTS, cols), bf16),
            jax.ShapeDtypeStruct((depth, width), f32),
        ),
        in_specs=[vmem] * 4,
        out_specs=(hbm, hbm),
        scratch_shapes=[
            pltpu.VMEM((pieces, 2, 128, cols), bf16),
            pltpu.VMEM((pieces, 2, 128, cols), bf16),
            pltpu.VMEM((pieces, SLOTS, cols), bf16),
            pltpu.VMEM((SLOTS, rows), bf16),
            pltpu.VMEM((SLOTS, SLOTS), bf16),
            pltpu.VMEM((7, depth, block), bf16),
            pltpu.VMEM((depth, block), f32),
            pltpu.VMEM((7, 8, block), f32),
            pltpu.VMEM((8, block), f32),
            dma((pieces,)), dma((pieces,)), dma((pieces,)), dma((pieces,)), dma((pieces,)), dma((pieces,)),
            dma((5,)), dma((5,)), dma(()),
        ],
        compiler_params=pltpu.CompilerParams(
            collective_id=0, has_side_effects=True, vmem_limit_bytes=48 * 1024 * 1024
        ),
        name="exchange",
    )(wiring.reshape(1, rows), send_grads, lagged_grads, weights)
    input_grads = pl.pallas_call(
        functools.partial(norm, pieces, cols),
        out_shape=jax.ShapeDtypeStruct((SLOTS, width), bf16),
        in_specs=[vmem] * 4,
        out_specs=vmem,
        scratch_shapes=[
            pltpu.VMEM((SLOTS, width), bf16),
            pltpu.VMEM((SLOTS, SLOTS), bf16),
        ],
        compiler_params=pltpu.CompilerParams(vmem_limit_bytes=48 * 1024 * 1024),
        name="norm",
    )(arrived, loss_grad, saved_acts, gain)
    return (input_grads, new_weights)


def solution(mesh):
    return jax.shard_map(
        per_device,
        mesh=mesh,
        in_specs=(
            P(("section", "peer"), None),
            P(("section", "peer"), None),
            P("peer", None),
            P(("section", "peer"), None),
            P("section", None),
            P("section", "peer"),
            P("section", None),
        ),
        out_specs=(P(("section", "peer"), None), P("section", None)),
        check_vma=False,
    )
```

```python
import functools

import jax
import jax.numpy as jnp
from jax import lax
from jax.experimental import pallas as pl
from jax.experimental.pallas import tpu as pltpu
from jax.sharding import PartitionSpec as P

MESH = pl.DeviceIdType.MESH
SLOTS = 256
CAP = 4
PIECES = 10
AHEAD = 3
LAG = 4


def place():
    s = lax.axis_index("section")
    p = lax.axis_index("peer")
    return s, p // 8, (p // 2) % 4, p % 2


def iota(shape, dim):
    return lax.broadcasted_iota(jnp.int32, shape, dim)


def slot_matrix(wire, z, y, h):
    rows = wire.shape[1]
    r, c = iota((rows, rows), 0), iota((rows, rows), 1)
    across = jnp.broadcast_to(wire, (rows, rows))
    down = jnp.sum(jnp.where(r == c, across, 0), axis=1, keepdims=True)
    rank = jnp.sum(jnp.where((down == across) & (r < c), 1, 0), axis=0, keepdims=True)
    key = wire * CAP + rank
    i = iota((SLOTS, rows), 0)
    dh, d, dy, k = i >> 7, (i >> 4) & 7, (i >> 2) & 3, i & 3
    q = ((z + d) & 7) * 8 + ((y + dy) & 3) * 2 + ((h + dh) & 1)
    return jnp.where(q * CAP + k == key, 1.0, 0.0).astype(jnp.bfloat16)


def regroup_matrix():
    o, i = iota((SLOTS, SLOTS), 0), iota((SLOTS, SLOTS), 1)
    dy, dh, d, k = o >> 6, (o >> 5) & 1, (o >> 2) & 7, o & 3
    return jnp.where(dh * 128 + d * 16 + dy * 4 + k == i, 1.0, 0.0).astype(jnp.bfloat16)


def natural_matrix(z, y, h):
    n, o = iota((SLOTS, SLOTS), 0), iota((SLOTS, SLOTS), 1)
    zs, ys, hs, k = n >> 5, (n >> 3) & 3, (n >> 2) & 1, n & 3
    d, dy, dh = (z - zs) & 7, (y - ys) & 3, (h - hs) & 1
    return jnp.where((dy * 2 + dh) * 32 + d * 4 + k == o, 1.0, 0.0).astype(jnp.bfloat16)


def exchange(pieces, cols, wire, gain, rows_hbm, lag_ref, w_ref, loss, acts_hbm, out_hbm, new_w,
             send1, recv1, send2, arrived, rows_ref, acts, grads, out, squares, products,
             slots, regroup, natural, lag_own, lag_in, part, part_in, fresh, w_own,
             s0, r0, s1, r1, s2, r2, sa, ra, local, row_sem, out_sem):
    s, z, y, h = place()
    width = lag_ref.shape[1]
    block = width // 8
    own = pl.ds(pl.multiple_of((y * 2 + h) * block, 128), block)
    zrows = pl.ds(pl.multiple_of(z * 8, 8), 8)

    def at(section, dz, dy, dh):
        peer = ((z + dz) % 8) * 8 + ((y + dy) % 4) * 2 + (h + dh) % 2
        return (section, peer)

    def push(src, dst, ssem, rsem, to):
        return pltpu.make_async_remote_copy(src_ref=src, dst_ref=dst, send_sem=ssem, recv_sem=rsem,
                                            device_id=to, device_id_type=MESH)

    me = at(s, 0, 0, 0)
    barrier = pltpu.get_barrier_semaphore()
    for d in range(1, 8):
        pl.semaphore_signal(barrier, inc=1, device_id=at(s, d, 0, 0), device_id_type=MESH)
    for e in range(8):
        for ds in range(4):
            if e or ds:
                pl.semaphore_signal(barrier, inc=1, device_id=at((s + ds) % 4, 0, e // 2, e % 2), device_id_type=MESH)

    crossing = lambda i: lax.rem(i, 2) == 1

    def span(i):
        return pl.ds(pl.multiple_of(i * cols, 128), cols)

    def fetch(i):
        return pltpu.make_async_copy(rows_hbm.at[:, span(i)], rows_ref.at[:, span(i)], row_sem.at[i])

    fetch_lag = pltpu.make_async_copy(lag_ref.at[:, own], lag_own, local.at[1])
    fetch_w = pltpu.make_async_copy(w_ref.at[zrows, own], w_own, local.at[2])
    fetch_acts = pltpu.make_async_copy(acts_hbm, acts, local.at[3])
    fetch_loss = pltpu.make_async_copy(loss, grads, local.at[4])

    @pl.when(s >= 1)
    def _():
        for i in range(pieces):
            fetch(i).start()

    fetch_lag.start()
    fetch_w.start()
    fetch_acts.start()
    pl.when(s == 3)(fetch_loss.start)
    squares[...] = jnp.zeros_like(squares)
    products[...] = jnp.zeros_like(products)

    slots[...] = slot_matrix(wire[...], z, y, h)

    def arrange(i):
        fetch(i).wait()
        data = jnp.dot(slots[...], rows_ref[:, span(i)], preferred_element_type=jnp.float32).astype(jnp.bfloat16)
        data = data.reshape(2, 128, cols)
        send1[i] = data
        recv1[i, :, 0:16, :] = data[:, 0:16, :]

    pl.when(s >= 1)(lambda: arrange(0))
    pl.semaphore_wait(barrier, 38)

    def lag_copy(e):
        dy, dh = e // 2, e % 2
        j = ((y + dy) % 4) * 2 + (h + dh) % 2
        return push(lag_ref.at[:, pl.ds(pl.multiple_of(j * block, 128), block)], lag_in.at[e - 1], sa.at[0], ra.at[0],
                    at(s, 0, dy, dh))

    for e in range(1, 8):
        lag_copy(e).start()

    def along_z(i, d):
        lines = pl.ds(d * 16, 16)
        return push(send1.at[i, :, lines, :], recv1.at[i, :, lines, :], s1.at[i], r1.at[i], at(s, d, 0, 0))

    def along_z_all(i):
        lines = pl.ds(16, 112)
        return push(send1.at[i, :, lines, :], recv1.at[i, :, lines, :], s1.at[i], r1.at[i], at(s, 1, 0, 0))

    def start_z(i):
        for d in (4, 3, 5, 2, 6, 1, 7):
            along_z(i, d).start()

    def cross(i, dh, first):
        lines = pl.ds(0, 16) if first else pl.ds(16, 112)
        return push(send1.at[i, dh, lines, :], (recv1 if first else send1).at[i, dh, lines, :],
                    s0.at[i], r0.at[i], at(0, 0, 0, dh))

    def whole(buffer, i, ssem, rsem):
        return push(buffer.at[i], buffer.at[i], ssem.at[i], rsem.at[i], at((s + 3) % 4, 0, 0, 0))

    def start_out(i, carry):
        @pl.when((s == 1) | (s == 3) | ((s == 2) & ~crossing(i)))
        def _():
            start_z(i)

        @pl.when((s == 2) & crossing(i))
        def _():
            for dh in range(2):
                cross(i, dh, False).start()
                cross(i, dh, True).start()

        return carry

    start_out(0, 0)

    @pl.when(s >= 1)
    def _():
        def arrange_start(i, carry):
            arrange(i)
            pl.when(i < AHEAD)(lambda: (start_out(i, 0), None)[1])
            return carry
        lax.fori_loop(1, pieces, arrange_start, 0)

    regroup[...] = regroup_matrix()
    natural[...] = natural_matrix(z, y, h)
    fetch_acts.wait()
    pl.when(s == 3)(fetch_loss.wait)

    def onward(i):
        whole(send2, i, s0, r0).wait_recv()
        start_z(i)

    @pl.when(s == 0)
    def _():
        onward(1)

    def lag_sum():
        push(lag_in, lag_in, sa.at[0], ra.at[0], me).wait_recv()
        fetch_lag.wait()
        total = lag_own[...].astype(jnp.float32)
        for e in range(7):
            total = total + lag_in[e].astype(jnp.float32)
        part[...] = total
        for d in range(1, 8):
            to = (z + d) % 8
            push(part.at[pl.ds(pl.multiple_of(to * 8, 8), 8)], part_in.at[d - 1], sa.at[1], ra.at[1],
                 at(s, d, 0, 0)).start()

    def update():
        push(part_in, part_in, sa.at[1], ra.at[1], me).wait_recv()
        total = part[zrows, :]
        for d in range(7):
            total = total + part_in[d]
        fetch_w.wait()
        fresh[...] = w_own[...] - 0.5 * (total / 64.0)
        for d in range(1, 8):
            push(fresh, new_w.at[zrows, own], sa.at[2], ra.at[2], at(s, d, 0, 0)).start()
        pltpu.make_async_copy(fresh, new_w.at[zrows, own], local.at[0]).start()

    def gather_h():
        push(part_in, part_in, sa.at[2], ra.at[2], me).wait_recv()
        pltpu.make_async_copy(fresh, new_w.at[zrows, own], local.at[0]).wait()
        push(new_w.at[:, own], new_w.at[:, own], sa.at[3], ra.at[3], at(s, 0, 0, 1)).start()

    pair = pl.ds(pl.multiple_of(y * 2 * block, 128), 2 * block)

    def gather_y():
        push(part, part, sa.at[3], ra.at[3], me).wait_recv()
        for dy in (2, 1, 3):
            push(new_w.at[:, pair], new_w.at[:, pair], sa.at[4], ra.at[4], at(s, 0, dy, 0)).start()

    three = pl.ds(0, 6 * block)

    def relay(i):
        data = recv1[i].reshape(SLOTS, cols)
        send2[i] = jnp.dot(regroup[...], data, preferred_element_type=jnp.float32).astype(jnp.bfloat16)

        @pl.when(s >= 1)
        def _():
            for e in (4, 5, 2, 3, 6, 7, 1, 0):
                lines = pl.ds(e * 32, 32)
                push(send2.at[i, lines, :], arrived.at[i, lines, :], s2.at[i], r2.at[i],
                     at((s + 3) % 4, 0, e // 2, e % 2)).start()

        @pl.when(s == 0)
        def _():
            for dy in (2, 1, 3, 0):
                lines = pl.ds(dy * 64, 64)
                push(send2.at[i, lines, :], arrived.at[i, lines, :], s2.at[i], r2.at[i], at(1, 0, dy, 0)).start()

    def squared(i):
        x = acts[:, span(i)].astype(jnp.float32)
        products_x = x * x
        total = squares[...]
        for c in range(cols // 128):
            total = total + products_x[:, c * 128:(c + 1) * 128]
        squares[...] = total

    def multiplied(i, g):
        terms = g * gain[:, span(i)] * acts[:, span(i)].astype(jnp.float32)
        total = products[...]
        for c in range(cols // 128):
            total = total + terms[:, c * 128:(c + 1) * 128]
        products[...] = total

    def take(i):
        whole(arrived, i, s2, r2).wait_recv()
        g = jnp.dot(natural[...], arrived[i], preferred_element_type=jnp.float32)
        grads[:, span(i)] = g.astype(jnp.bfloat16)
        multiplied(i, g)

    relays = lambda i: (s == 1) | (s == 3) | ((s == 2) & ~crossing(i)) | ((s == 0) & crossing(i))

    def step(i, carry):
        pl.when(i == 1)(lag_sum)
        pl.when(i == 3)(update)
        pl.when(i == 5)(gather_h)
        pl.when(i == 6)(gather_y)
        pl.when(relays(i))(lambda: along_z_all(i).wait_recv())
        pl.when((s == 0) & ~crossing(i) & (i + 3 < pieces))(lambda: onward(i + 3))
        pl.when(i + AHEAD < pieces)(lambda: (start_out(i + AHEAD, 0), None)[1])
        pl.when(relays(i))(lambda: relay(i))
        squared(i)
        pl.when(s == 3)(lambda: multiplied(i, grads[:, span(i)].astype(jnp.float32)))
        pl.when((s < 3) & (i >= LAG))(lambda: take(i - LAG))
        return carry

    lax.fori_loop(0, pieces, step, 0)

    @pl.when(s < 3)
    def _():
        lax.fori_loop(pieces - LAG, pieces, lambda i, carry: (take(i), carry)[1], 0)

    def emit(b):
        rows = pl.ds(pl.multiple_of(b * 32, 32), 32)
        return pltpu.make_async_copy(out.at[rows, :], out_hbm.at[rows, :], out_sem.at[b])

    def last(b, carry):
        for part_of in range(2):
            rows = pl.ds(pl.multiple_of(b * 32 + part_of * 16, 16), 16)
            r = lax.rsqrt(jnp.sum(squares[rows, :], axis=1, keepdims=True) / width + 1e-05)
            inner = jnp.sum(products[rows, :], axis=1, keepdims=True) * r / width
            for c in range(pieces):
                at_cols = slice(c * cols, (c + 1) * cols)
                x = acts[rows, at_cols].astype(jnp.float32)
                g = grads[rows, at_cols].astype(jnp.float32)
                out[rows, at_cols] = (g + (g * gain[:, at_cols] - (x * r) * inner) * r).astype(jnp.bfloat16)
        emit(b).start()
        return carry

    lax.fori_loop(0, SLOTS // 32, last, 0)

    def finish(i, carry):
        @pl.when(relays(i))
        def _():
            along_z_all(i).wait_send()
            whole(send2, i, s2, r2).wait_send()

        @pl.when((s == 2) & crossing(i))
        def _():
            whole(send2, i, s0, r0).wait_send()

        return carry

    lax.fori_loop(0, pieces, finish, 0)
    push(lag_in, lag_in, sa.at[0], ra.at[0], me).wait_send()
    push(part_in, part_in, sa.at[1], ra.at[1], me).wait_send()
    push(part_in, part_in, sa.at[2], ra.at[2], me).wait_send()
    push(part, part, sa.at[3], ra.at[3], me).wait_send()
    push(new_w.at[:, three], new_w.at[:, three], sa.at[4], ra.at[4], me).wait()
    lax.fori_loop(0, SLOTS // 32, lambda b, carry: (emit(b).wait(), carry)[1], 0)


def per_device(send_grads, wiring, loss_grad, saved_acts, gain, lagged_grads, weights):
    rows, width = send_grads.shape
    pieces, cols = PIECES, width // PIECES
    depth = lagged_grads.shape[0]
    block = width // 8
    vmem = pl.BlockSpec(memory_space=pltpu.VMEM)
    hbm = pl.BlockSpec(memory_space=pl.ANY)
    bf16, f32 = jnp.bfloat16, jnp.float32
    dma = pltpu.SemaphoreType.DMA
    return pl.pallas_call(
        functools.partial(exchange, pieces, cols),
        out_shape=(
            jax.ShapeDtypeStruct((SLOTS, width), bf16),
            jax.ShapeDtypeStruct((depth, width), f32),
        ),
        in_specs=[vmem] * 2 + [hbm] * 5,
        out_specs=(hbm, hbm),
        scratch_shapes=[
            pltpu.VMEM((pieces, 2, 128, cols), bf16),
            pltpu.VMEM((pieces, 2, 128, cols), bf16),
            pltpu.VMEM((pieces, SLOTS, cols), bf16),
            pltpu.VMEM((pieces, SLOTS, cols), bf16),
            pltpu.VMEM((rows, width), bf16),
            pltpu.VMEM((SLOTS, width), bf16),
            pltpu.VMEM((SLOTS, width), bf16),
            pltpu.VMEM((SLOTS, width), bf16),
            pltpu.VMEM((SLOTS, 128), f32),
            pltpu.VMEM((SLOTS, 128), f32),
            pltpu.VMEM((SLOTS, rows), bf16),
            pltpu.VMEM((SLOTS, SLOTS), bf16),
            pltpu.VMEM((SLOTS, SLOTS), bf16),
            pltpu.VMEM((depth, block), bf16),
            pltpu.VMEM((7, depth, block), bf16),
            pltpu.VMEM((depth, block), f32),
            pltpu.VMEM((7, 8, block), f32),
            pltpu.VMEM((8, block), f32),
            pltpu.VMEM((8, block), f32),
            dma((pieces,)), dma((pieces,)), dma((pieces,)), dma((pieces,)), dma((pieces,)), dma((pieces,)),
            dma((5,)), dma((5,)), dma((5,)), dma((pieces,)), dma((SLOTS // 32,)),
        ],
        compiler_params=pltpu.CompilerParams(
            collective_id=0, has_side_effects=True, vmem_limit_bytes=60 * 1024 * 1024
        ),
        name="exchange",
    )(wiring.reshape(1, rows), gain, send_grads, lagged_grads, weights, loss_grad, saved_acts)


def solution(mesh):
    return jax.shard_map(
        per_device,
        mesh=mesh,
        in_specs=(
            P(("section", "peer"), None),
            P(("section", "peer"), None),
            P("peer", None),
            P(("section", "peer"), None),
            P("section", None),
            P("section", "peer"),
            P("section", None),
        ),
        out_specs=(P(("section", "peer"), None), P("section", None)),
        check_vma=False,
    )
```

```python
import functools

import jax
import jax.numpy as jnp
from jax import lax
from jax.experimental import pallas as pl
from jax.experimental.pallas import tpu as pltpu
from jax.sharding import PartitionSpec as P

MESH = pl.DeviceIdType.MESH
SLOTS = 256
CAP = 4
PIECES = 10
AHEAD = 3
LAG = 4


def place():
    s = lax.axis_index("section")
    p = lax.axis_index("peer")
    return s, p // 8, (p // 2) % 4, p % 2


def iota(shape, dim):
    return lax.broadcasted_iota(jnp.int32, shape, dim)


def slot_matrix(wire, z, y, h):
    rows = wire.shape[1]
    r, c = iota((rows, rows), 0), iota((rows, rows), 1)
    across = jnp.broadcast_to(wire, (rows, rows))
    down = jnp.sum(jnp.where(r == c, across, 0), axis=1, keepdims=True)
    rank = jnp.sum(jnp.where((down == across) & (r < c), 1, 0), axis=0, keepdims=True)
    key = wire * CAP + rank
    i = iota((SLOTS, rows), 0)
    dh, d, dy, k = i >> 7, (i >> 4) & 7, (i >> 2) & 3, i & 3
    q = ((z + d) & 7) * 8 + ((y + dy) & 3) * 2 + ((h + dh) & 1)
    return jnp.where(q * CAP + k == key, 1.0, 0.0).astype(jnp.bfloat16)


def regroup_matrix():
    o, i = iota((SLOTS, SLOTS), 0), iota((SLOTS, SLOTS), 1)
    dy, dh, d, k = o >> 6, (o >> 5) & 1, (o >> 2) & 7, o & 3
    return jnp.where(dh * 128 + d * 16 + dy * 4 + k == i, 1.0, 0.0).astype(jnp.bfloat16)


def natural_matrix(z, y, h):
    n, o = iota((SLOTS, SLOTS), 0), iota((SLOTS, SLOTS), 1)
    zs, ys, hs, k = n >> 5, (n >> 3) & 3, (n >> 2) & 1, n & 3
    d, dy, dh = (z - zs) & 7, (y - ys) & 3, (h - hs) & 1
    return jnp.where((dy * 2 + dh) * 32 + d * 4 + k == o, 1.0, 0.0).astype(jnp.bfloat16)


def exchange(pieces, cols, wire_hbm, gain_hbm, rows_hbm, lag_ref, w_ref, loss, acts_hbm, new_w, grads_hbm, squares, products,
             send1, recv1, send2, middle, arrived, rows_ref, acts, grads, wire, gain,
             slots, regroup, natural, lag_own, lag_in, part, part_in, fresh, w_own,
             s0, r0, s1, r1, s2, r2, s3, r3, sa, ra, local, row_sem, out_sem):
    s, z, y, h = place()
    width = lag_ref.shape[1]
    block = width // 8
    own = pl.ds(pl.multiple_of((y * 2 + h) * block, 128), block)
    zrows = pl.ds(pl.multiple_of(z * 8, 8), 8)

    def at(section, dz, dy, dh):
        peer = ((z + dz) % 8) * 8 + ((y + dy) % 4) * 2 + (h + dh) % 2
        return (section, peer)

    def push(src, dst, ssem, rsem, to):
        return pltpu.make_async_remote_copy(src_ref=src, dst_ref=dst, send_sem=ssem, recv_sem=rsem,
                                            device_id=to, device_id_type=MESH)

    me = at(s, 0, 0, 0)
    barrier = pltpu.get_barrier_semaphore()
    for d in range(1, 8):
        pl.semaphore_signal(barrier, inc=1, device_id=at(s, d, 0, 0), device_id_type=MESH)
    for e in range(8):
        for ds in range(4):
            if e or ds:
                pl.semaphore_signal(barrier, inc=1, device_id=at((s + ds) % 4, 0, e // 2, e % 2), device_id_type=MESH)

    crossing = lambda i: lax.rem(i, 2) == 1

    def span(i):
        return pl.ds(pl.multiple_of(i * cols, 128), cols)

    def fetch(i):
        return pltpu.make_async_copy(rows_hbm.at[:, span(i)], rows_ref.at[:, span(i)], row_sem.at[i])

    fetch_lag = pltpu.make_async_copy(lag_ref.at[:, own], lag_own, local.at[1])
    fetch_w = pltpu.make_async_copy(w_ref.at[zrows, own], w_own, local.at[2])
    fetch_acts = pltpu.make_async_copy(acts_hbm, acts, local.at[3])
    fetch_wire = pltpu.make_async_copy(wire_hbm, wire, local.at[5])
    fetch_gain = pltpu.make_async_copy(gain_hbm, gain, local.at[6])
    fetch_loss = pltpu.make_async_copy(loss, grads, local.at[4])

    fetch_wire.start()

    @pl.when(s >= 1)
    def _():
        for i in range(pieces):
            fetch(i).start()

    fetch_lag.start()
    fetch_gain.start()
    fetch_w.start()
    fetch_acts.start()
    pl.when(s == 3)(fetch_loss.start)
    squares[...] = jnp.zeros_like(squares)
    products[...] = jnp.zeros_like(products)

    fetch_wire.wait()
    slots[...] = slot_matrix(wire[...], z, y, h)

    def arrange(i):
        fetch(i).wait()
        data = jnp.dot(slots[...], rows_ref[:, span(i)], preferred_element_type=jnp.float32).astype(jnp.bfloat16)
        data = data.reshape(2, 128, cols)
        send1[i] = data
        recv1[i, :, 0:16, :] = data[:, 0:16, :]

    pl.when(s >= 1)(lambda: arrange(0))
    pl.semaphore_wait(barrier, 38)

    def lag_copy(e):
        dy, dh = e // 2, e % 2
        j = ((y + dy) % 4) * 2 + (h + dh) % 2
        return push(lag_ref.at[:, pl.ds(pl.multiple_of(j * block, 128), block)], lag_in.at[e - 1], sa.at[0], ra.at[0],
                    at(s, 0, dy, dh))

    for e in range(1, 8):
        lag_copy(e).start()

    def along_z(i, d):
        lines = pl.ds(d * 16, 16)
        return push(send1.at[i, :, lines, :], recv1.at[i, :, lines, :], s1.at[i], r1.at[i], at(s, d, 0, 0))

    def along_z_all(i):
        lines = pl.ds(16, 112)
        return push(send1.at[i, :, lines, :], recv1.at[i, :, lines, :], s1.at[i], r1.at[i], at(s, 1, 0, 0))

    def start_z(i):
        for d in (4, 3, 5, 2, 6, 1, 7):
            along_z(i, d).start()

    def cross(i, dh, first):
        lines = pl.ds(0, 16) if first else pl.ds(16, 112)
        return push(send1.at[i, dh, lines, :], (recv1 if first else send1).at[i, dh, lines, :],
                    s0.at[i], r0.at[i], at(0, 0, 0, dh))

    def whole(buffer, i, ssem, rsem):
        return push(buffer.at[i], buffer.at[i], ssem.at[i], rsem.at[i], at((s + 3) % 4, 0, 0, 0))

    def start_out(i, carry):
        @pl.when((s == 1) | (s == 3) | ((s == 2) & ~crossing(i)))
        def _():
            start_z(i)

        @pl.when((s == 2) & crossing(i))
        def _():
            for dh in range(2):
                cross(i, dh, False).start()
                cross(i, dh, True).start()

        return carry

    start_out(0, 0)

    @pl.when(s >= 1)
    def _():
        def arrange_start(i, carry):
            arrange(i)
            pl.when(i < AHEAD)(lambda: (start_out(i, 0), None)[1])
            return carry
        lax.fori_loop(1, pieces, arrange_start, 0)

    regroup[...] = regroup_matrix()
    natural[...] = natural_matrix(z, y, h)
    fetch_acts.wait()
    fetch_gain.wait()
    pl.when(s == 3)(fetch_loss.wait)

    def onward(i):
        whole(send2, i, s0, r0).wait_recv()
        start_z(i)

    @pl.when(s == 0)
    def _():
        onward(1)

    def lag_sum():
        push(lag_in, lag_in, sa.at[0], ra.at[0], me).wait_recv()
        fetch_lag.wait()
        total = lag_own[...].astype(jnp.float32)
        for e in range(7):
            total = total + lag_in[e].astype(jnp.float32)
        part[...] = total
        for d in range(1, 8):
            to = (z + d) % 8
            push(part.at[pl.ds(pl.multiple_of(to * 8, 8), 8)], part_in.at[d - 1], sa.at[1], ra.at[1],
                 at(s, d, 0, 0)).start()

    def update():
        push(part_in, part_in, sa.at[1], ra.at[1], me).wait_recv()
        total = part[zrows, :]
        for d in range(7):
            total = total + part_in[d]
        fetch_w.wait()
        fresh[...] = w_own[...] - 0.5 * (total / 64.0)
        for d in range(1, 8):
            push(fresh, new_w.at[zrows, own], sa.at[2], ra.at[2], at(s, d, 0, 0)).start()
        pltpu.make_async_copy(fresh, new_w.at[zrows, own], local.at[0]).start()

    def gather_h():
        push(part_in, part_in, sa.at[2], ra.at[2], me).wait_recv()
        pltpu.make_async_copy(fresh, new_w.at[zrows, own], local.at[0]).wait()
        push(new_w.at[:, own], new_w.at[:, own], sa.at[3], ra.at[3], at(s, 0, 0, 1)).start()

    pair = pl.ds(pl.multiple_of(y * 2 * block, 128), 2 * block)

    def gather_y():
        push(part, part, sa.at[3], ra.at[3], me).wait_recv()
        for dy in (2, 1, 3):
            push(new_w.at[:, pair], new_w.at[:, pair], sa.at[4], ra.at[4], at(s, 0, dy, 0)).start()

    three = pl.ds(0, 6 * block)

    def relay(i):
        data = jnp.dot(regroup[...], recv1[i].reshape(SLOTS, cols), preferred_element_type=jnp.float32)
        data = data.astype(jnp.bfloat16).reshape(4, 64, cols)
        send2[i] = data

        @pl.when((s == 1) | (s == 3))
        def _():
            for dy, dh in ((2, 0), (2, 1), (1, 0), (1, 1), (3, 0), (3, 1), (0, 1), (0, 0)):
                lines = pl.ds(dh * 32, 32)
                push(send2.at[i, dy, lines, :], arrived.at[i, dy, lines, :], s2.at[i], r2.at[i],
                     at(s - 1, 0, dy, dh)).start()

        @pl.when(s == 2)
        def _():
            middle[i, 0] = data[0]
            for dy in (2, 1, 3):
                push(send2.at[i, dy], middle.at[i, dy], s3.at[i], r3.at[i], at(2, 0, dy, 0)).start()

        @pl.when(s == 0)
        def _():
            for dy in (2, 1, 3, 0):
                push(send2.at[i, dy], arrived.at[i, dy], s2.at[i], r2.at[i], at(1, 0, dy, 0)).start()

    def three_rows(i):
        rows = pl.ds(1, 3)
        return push(send2.at[i, rows], middle.at[i, rows], s3.at[i], r3.at[i], at(2, 0, 1, 0))

    def forward(i):
        three_rows(i).wait_recv()
        for dh in (1, 0):
            lines = pl.ds(dh * 32, 32)
            push(middle.at[i, :, lines, :], arrived.at[i, :, lines, :], s2.at[i], r2.at[i], at(1, 0, 0, dh)).start()

    def squared(i):
        x = acts[:, span(i)].astype(jnp.float32)
        products_x = x * x
        total = squares[...]
        for c in range(cols // 128):
            total = total + products_x[:, c * 128:(c + 1) * 128]
        squares[...] = total

    def multiplied(i, g):
        terms = g * gain[:, span(i)] * acts[:, span(i)].astype(jnp.float32)
        total = products[...]
        for c in range(cols // 128):
            total = total + terms[:, c * 128:(c + 1) * 128]
        products[...] = total

    def keep(i):
        return pltpu.make_async_copy(grads.at[:, span(i)], grads_hbm.at[:, span(i)], out_sem.at[i])

    def take_loss(i):
        keep(i).start()
        multiplied(i, grads[:, span(i)].astype(jnp.float32))

    def take(i):
        whole(arrived, i, s2, r2).wait_recv()
        g = jnp.dot(natural[...], arrived[i].reshape(SLOTS, cols), preferred_element_type=jnp.float32)
        grads[:, span(i)] = g.astype(jnp.bfloat16)
        keep(i).start()
        multiplied(i, g)

    relays = lambda i: (s == 1) | (s == 3) | ((s == 2) & ~crossing(i)) | ((s == 0) & crossing(i))

    def step(i, carry):
        pl.when(i == 1)(lag_sum)
        pl.when(i == 3)(update)
        pl.when(i == 5)(gather_h)
        pl.when(i == 6)(gather_y)
        pl.when(relays(i))(lambda: along_z_all(i).wait_recv())
        pl.when((s == 0) & ~crossing(i) & (i + 3 < pieces))(lambda: onward(i + 3))
        pl.when(i + AHEAD < pieces)(lambda: (start_out(i + AHEAD, 0), None)[1])
        pl.when(relays(i))(lambda: relay(i))
        pl.when((s == 2) & crossing(i))(lambda: forward(i - 1))
        squared(i)
        pl.when(s == 3)(lambda: take_loss(i))
        pl.when((s < 3) & (i >= LAG))(lambda: take(i - LAG))
        return carry

    lax.fori_loop(0, pieces, step, 0)

    @pl.when(s < 3)
    def _():
        lax.fori_loop(pieces - LAG, pieces, lambda i, carry: (take(i), carry)[1], 0)

    def finish(i, carry):
        @pl.when(relays(i))
        def _():
            along_z_all(i).wait_send()
            whole(send2, i, s2, r2).wait_send()

        pl.when((s == 2) & ~crossing(i))(lambda: three_rows(i).wait_send())

        @pl.when((s == 2) & crossing(i))
        def _():
            whole(send2, i, s0, r0).wait_send()

        return carry

    lax.fori_loop(0, pieces, finish, 0)
    push(lag_in, lag_in, sa.at[0], ra.at[0], me).wait_send()
    push(part_in, part_in, sa.at[1], ra.at[1], me).wait_send()
    push(part_in, part_in, sa.at[2], ra.at[2], me).wait_send()
    push(part, part, sa.at[3], ra.at[3], me).wait_send()
    push(new_w.at[:, three], new_w.at[:, three], sa.at[4], ra.at[4], me).wait()
    lax.fori_loop(0, pieces, lambda i, carry: (keep(i).wait(), carry)[1], 0)


def norm(cols, gain_hbm, acts_hbm, grads_hbm, squares_hbm, products_hbm, fresh, out_hbm, new_w,
         gain, acts, grads, squares, products, out, held, small, acts_sem, grads_sem, out_sem):
    width = acts.shape[1]
    blocks = SLOTS // 32

    def lines(b):
        return pl.ds(pl.multiple_of(b * 32, 32), 32)

    def fetch_acts(b):
        return pltpu.make_async_copy(acts_hbm.at[lines(b), :], acts.at[lines(b), :], acts_sem.at[b])

    def fetch_grads(b):
        return pltpu.make_async_copy(grads_hbm.at[lines(b), :], grads.at[lines(b), :], grads_sem.at[b])

    def emit(b):
        return pltpu.make_async_copy(out.at[lines(b), :], out_hbm.at[lines(b), :], out_sem.at[b])

    firsts = [
        pltpu.make_async_copy(src, dst, small.at[n])
        for n, (src, dst) in enumerate(((gain_hbm, gain), (squares_hbm, squares), (products_hbm, products)))
    ]
    fetch_w = pltpu.make_async_copy(fresh, held, small.at[3])
    pass_on = pltpu.make_async_copy(held, new_w, small.at[4])
    for copy in firsts:
        copy.start()
    for b in range(blocks):
        fetch_acts(b).start()
        fetch_grads(b).start()
    fetch_w.start()
    for copy in firsts:
        copy.wait()

    def last(b, carry):
        fetch_acts(b).wait()
        fetch_grads(b).wait()
        for half in range(2):
            rows = pl.ds(pl.multiple_of(b * 32 + half * 16, 16), 16)
            r = lax.rsqrt(jnp.sum(squares[rows, :], axis=1, keepdims=True) / width + 1e-05)
            inner = jnp.sum(products[rows, :], axis=1, keepdims=True) * r / width
            for c in range(0, width, cols):
                at_cols = slice(c, c + cols)
                x = acts[rows, at_cols].astype(jnp.float32)
                g = grads[rows, at_cols].astype(jnp.float32)
                out[rows, at_cols] = (g + (g * gain[:, at_cols] - (x * r) * inner) * r).astype(jnp.bfloat16)
        emit(b).start()
        return carry

    lax.fori_loop(0, blocks // 2, last, 0)
    fetch_w.wait()
    pass_on.start()
    lax.fori_loop(blocks // 2, blocks, last, 0)
    lax.fori_loop(0, blocks, lambda b, carry: (emit(b).wait(), carry)[1], 0)
    pass_on.wait()


def per_device(send_grads, wiring, loss_grad, saved_acts, gain, lagged_grads, weights):
    rows, width = send_grads.shape
    pieces, cols = PIECES, width // PIECES
    depth = lagged_grads.shape[0]
    block = width // 8
    vmem = pl.BlockSpec(memory_space=pltpu.VMEM)
    hbm = pl.BlockSpec(memory_space=pl.ANY)
    bf16, f32 = jnp.bfloat16, jnp.float32
    dma = pltpu.SemaphoreType.DMA
    fresh, grads, squares, products = pl.pallas_call(
        functools.partial(exchange, pieces, cols),
        out_shape=(
            jax.ShapeDtypeStruct((depth, width), f32),
            jax.ShapeDtypeStruct((SLOTS, width), bf16),
            jax.ShapeDtypeStruct((SLOTS, 128), f32),
            jax.ShapeDtypeStruct((SLOTS, 128), f32),
        ),
        in_specs=[hbm] * 7,
        out_specs=(hbm, hbm, vmem, vmem),
        scratch_shapes=[
            pltpu.VMEM((pieces, 2, 128, cols), bf16),
            pltpu.VMEM((pieces, 2, 128, cols), bf16),
            pltpu.VMEM((pieces, 4, 64, cols), bf16),
            pltpu.VMEM((pieces, 4, 64, cols), bf16),
            pltpu.VMEM((pieces, 4, 64, cols), bf16),
            pltpu.VMEM((rows, width), bf16),
            pltpu.VMEM((SLOTS, width), bf16),
            pltpu.VMEM((SLOTS, width), bf16),
            pltpu.VMEM((1, rows), jnp.int32),
            pltpu.VMEM((1, width), f32),
            pltpu.VMEM((SLOTS, rows), bf16),
            pltpu.VMEM((SLOTS, SLOTS), bf16),
            pltpu.VMEM((SLOTS, SLOTS), bf16),
            pltpu.VMEM((depth, block), bf16),
            pltpu.VMEM((7, depth, block), bf16),
            pltpu.VMEM((depth, block), f32),
            pltpu.VMEM((7, 8, block), f32),
            pltpu.VMEM((8, block), f32),
            pltpu.VMEM((8, block), f32),
            dma((pieces,)), dma((pieces,)), dma((pieces,)), dma((pieces,)), dma((pieces,)), dma((pieces,)),
            dma((pieces,)), dma((pieces,)), dma((5,)), dma((5,)), dma((7,)), dma((pieces,)), dma((pieces,)),
        ],
        compiler_params=pltpu.CompilerParams(
            collective_id=0, has_side_effects=True, vmem_limit_bytes=59 * 1024 * 1024
        ),
        name="exchange",
    )(wiring.reshape(1, rows), gain, send_grads, lagged_grads, weights, loss_grad, saved_acts)
    return pl.pallas_call(
        functools.partial(norm, 512),
        out_shape=(
            jax.ShapeDtypeStruct((SLOTS, width), bf16),
            jax.ShapeDtypeStruct((depth, width), f32),
        ),
        in_specs=[hbm] * 6,
        out_specs=(hbm, hbm),
        scratch_shapes=[
            pltpu.VMEM((1, width), f32),
            pltpu.VMEM((SLOTS, width), bf16),
            pltpu.VMEM((SLOTS, width), bf16),
            pltpu.VMEM((SLOTS, 128), f32),
            pltpu.VMEM((SLOTS, 128), f32),
            pltpu.VMEM((SLOTS, width), bf16),
            pltpu.VMEM((depth, width), f32),
            dma((5,)), dma((SLOTS // 32,)), dma((SLOTS // 32,)), dma((SLOTS // 32,)),
        ],
        compiler_params=pltpu.CompilerParams(vmem_limit_bytes=59 * 1024 * 1024),
        name="norm",
    )(gain, saved_acts, grads, squares, products, fresh)


def solution(mesh):
    return jax.shard_map(
        per_device,
        mesh=mesh,
        in_specs=(
            P(("section", "peer"), None),
            P(("section", "peer"), None),
            P("peer", None),
            P(("section", "peer"), None),
            P("section", None),
            P("section", "peer"),
            P("section", None),
        ),
        out_specs=(P(("section", "peer"), None), P("section", None)),
        check_vma=False,
    )
```

```python
import functools

import jax
import jax.numpy as jnp
from jax import lax
from jax.experimental import pallas as pl
from jax.experimental.pallas import tpu as pltpu
from jax.sharding import PartitionSpec as P

MESH = pl.DeviceIdType.MESH
SLOTS = 256
CAP = 4
PIECES = 10
AHEAD = 3
LAG = 4


def place():
    s = lax.axis_index("section")
    p = lax.axis_index("peer")
    return s, p // 8, (p // 2) % 4, p % 2


def iota(shape, dim):
    return lax.broadcasted_iota(jnp.int32, shape, dim)


def slot_matrix(wire, z, y, h):
    rows = wire.shape[1]
    r, c = iota((rows, rows), 0), iota((rows, rows), 1)
    across = jnp.broadcast_to(wire, (rows, rows))
    down = jnp.sum(jnp.where(r == c, across, 0), axis=1, keepdims=True)
    rank = jnp.sum(jnp.where((down == across) & (r < c), 1, 0), axis=0, keepdims=True)
    key = wire * CAP + rank
    i = iota((SLOTS, rows), 0)
    dh, d, dy, k = i >> 7, (i >> 4) & 7, (i >> 2) & 3, i & 3
    q = ((z + d) & 7) * 8 + ((y + dy) & 3) * 2 + ((h + dh) & 1)
    return jnp.where(q * CAP + k == key, 1.0, 0.0).astype(jnp.bfloat16)


def regroup_matrix():
    o, i = iota((SLOTS, SLOTS), 0), iota((SLOTS, SLOTS), 1)
    dy, dh, d, k = o >> 6, (o >> 5) & 1, (o >> 2) & 7, o & 3
    return jnp.where(dh * 128 + d * 16 + dy * 4 + k == i, 1.0, 0.0).astype(jnp.bfloat16)


def natural_matrix(z, y, h):
    n, o = iota((SLOTS, SLOTS), 0), iota((SLOTS, SLOTS), 1)
    zs, ys, hs, k = n >> 5, (n >> 3) & 3, (n >> 2) & 1, n & 3
    d, dy, dh = (z - zs) & 7, (y - ys) & 3, (h - hs) & 1
    return jnp.where((dy * 2 + dh) * 32 + d * 4 + k == o, 1.0, 0.0).astype(jnp.bfloat16)


def exchange(pieces, cols, wire_hbm, gain_hbm, rows_hbm, lag_ref, w_ref, loss, acts_hbm, new_w, grads_hbm, squares, products,
             send1, recv1, send2, middle, arrived, rows_ref, acts, grads, wire, gain,
             slots, regroup, natural, lag_own, lag_in, part, part_in, fresh, w_own,
             s0, r0, s1, r1, s2, r2, s3, r3, sa, ra, local, row_sem, out_sem):
    s, z, y, h = place()
    width = lag_ref.shape[1]
    block = width // 8
    own = pl.ds(pl.multiple_of((y * 2 + h) * block, 128), block)
    zrows = pl.ds(pl.multiple_of(z * 8, 8), 8)

    def at(section, dz, dy, dh):
        peer = ((z + dz) % 8) * 8 + ((y + dy) % 4) * 2 + (h + dh) % 2
        return (section, peer)

    def push(src, dst, ssem, rsem, to):
        return pltpu.make_async_remote_copy(src_ref=src, dst_ref=dst, send_sem=ssem, recv_sem=rsem,
                                            device_id=to, device_id_type=MESH)

    me = at(s, 0, 0, 0)
    barrier = pltpu.get_barrier_semaphore()
    for d in range(1, 8):
        pl.semaphore_signal(barrier, inc=1, device_id=at(s, d, 0, 0), device_id_type=MESH)
    for e in range(8):
        for ds in range(4):
            if e or ds:
                pl.semaphore_signal(barrier, inc=1, device_id=at((s + ds) % 4, 0, e // 2, e % 2), device_id_type=MESH)

    crossing = lambda i: lax.rem(i, 2) == 1

    def span(i):
        return pl.ds(pl.multiple_of(i * cols, 128), cols)

    def fetch(i):
        return pltpu.make_async_copy(rows_hbm.at[:, span(i)], rows_ref.at[:, span(i)], row_sem.at[i])

    fetch_lag = pltpu.make_async_copy(lag_ref.at[:, own], lag_own, local.at[1])
    fetch_w = pltpu.make_async_copy(w_ref.at[zrows, own], w_own, local.at[2])
    fetch_acts = pltpu.make_async_copy(acts_hbm, acts, local.at[3])
    fetch_wire = pltpu.make_async_copy(wire_hbm, wire, local.at[5])
    fetch_gain = pltpu.make_async_copy(gain_hbm, gain, local.at[6])
    fetch_loss = pltpu.make_async_copy(loss, grads, local.at[4])

    fetch_wire.start()

    @pl.when(s >= 1)
    def _():
        for i in range(pieces):
            fetch(i).start()

    fetch_lag.start()
    fetch_gain.start()
    fetch_w.start()
    fetch_acts.start()
    pl.when(s == 3)(fetch_loss.start)
    squares[...] = jnp.zeros_like(squares)
    products[...] = jnp.zeros_like(products)

    fetch_wire.wait()
    slots[...] = slot_matrix(wire[...], z, y, h)

    def arrange(i):
        fetch(i).wait()
        data = jnp.dot(slots[...], rows_ref[:, span(i)], preferred_element_type=jnp.float32).astype(jnp.bfloat16)
        data = data.reshape(2, 128, cols)
        send1[i] = data
        recv1[i, :, 0:16, :] = data[:, 0:16, :]

    pl.when(s >= 1)(lambda: arrange(0))
    pl.semaphore_wait(barrier, 38)

    def lag_copy(e):
        dy, dh = e // 2, e % 2
        j = ((y + dy) % 4) * 2 + (h + dh) % 2
        return push(lag_ref.at[:, pl.ds(pl.multiple_of(j * block, 128), block)], lag_in.at[e - 1], sa.at[0], ra.at[0],
                    at(s, 0, dy, dh))

    for e in range(1, 8):
        lag_copy(e).start()

    def along_z(i, d):
        lines = pl.ds(d * 16, 16)
        return push(send1.at[i, :, lines, :], recv1.at[i, :, lines, :], s1.at[i], r1.at[i], at(s, d, 0, 0))

    def along_z_all(i):
        lines = pl.ds(16, 112)
        return push(send1.at[i, :, lines, :], recv1.at[i, :, lines, :], s1.at[i], r1.at[i], at(s, 1, 0, 0))

    def start_z(i):
        for d in (4, 3, 5, 2, 6, 1, 7):
            along_z(i, d).start()

    def cross(i, dh, first):
        lines = pl.ds(0, 16) if first else pl.ds(16, 112)
        return push(send1.at[i, dh, lines, :], (recv1 if first else send1).at[i, dh, lines, :],
                    s0.at[i], r0.at[i], at(0, 0, 0, dh))

    def whole(buffer, i, ssem, rsem):
        return push(buffer.at[i], buffer.at[i], ssem.at[i], rsem.at[i], at((s + 3) % 4, 0, 0, 0))

    def start_out(i, carry):
        @pl.when((s == 1) | (s == 3) | ((s == 2) & ~crossing(i)))
        def _():
            start_z(i)

        @pl.when((s == 2) & crossing(i))
        def _():
            for dh in range(2):
                cross(i, dh, False).start()
                cross(i, dh, True).start()

        return carry

    start_out(0, 0)

    @pl.when(s >= 1)
    def _():
        def arrange_start(i, carry):
            arrange(i)
            pl.when(i < AHEAD)(lambda: (start_out(i, 0), None)[1])
            return carry
        lax.fori_loop(1, pieces, arrange_start, 0)

    regroup[...] = regroup_matrix()
    natural[...] = natural_matrix(z, y, h)
    fetch_acts.wait()
    fetch_gain.wait()
    pl.when(s == 3)(fetch_loss.wait)

    def onward(i):
        whole(send2, i, s0, r0).wait_recv()
        start_z(i)

    @pl.when(s == 0)
    def _():
        onward(1)

    def lag_sum():
        push(lag_in, lag_in, sa.at[0], ra.at[0], me).wait_recv()
        fetch_lag.wait()
        total = lag_own[...].astype(jnp.float32)
        for e in range(7):
            total = total + lag_in[e].astype(jnp.float32)
        part[...] = total
        for d in range(1, 8):
            to = (z + d) % 8
            push(part.at[pl.ds(pl.multiple_of(to * 8, 8), 8)], part_in.at[d - 1], sa.at[1], ra.at[1],
                 at(s, d, 0, 0)).start()

    def update():
        push(part_in, part_in, sa.at[1], ra.at[1], me).wait_recv()
        total = part[zrows, :]
        for d in range(7):
            total = total + part_in[d]
        fetch_w.wait()
        fresh[...] = w_own[...] - 0.5 * (total / 64.0)
        for d in range(1, 8):
            push(fresh, new_w.at[zrows, own], sa.at[2], ra.at[2], at(s, d, 0, 0)).start()
        pltpu.make_async_copy(fresh, new_w.at[zrows, own], local.at[0]).start()

    half = new_w.shape[0] // 2
    upper, lower = pl.ds(0, half), pl.ds(half, half)
    pair = pl.ds(pl.multiple_of(y * 2 * block, 128), 2 * block)

    def columns(n):
        return new_w.at[upper, pl.ds(0, n * block)]

    def gather_first():
        push(part_in, part_in, sa.at[2], ra.at[2], me).wait_recv()
        pltpu.make_async_copy(fresh, new_w.at[zrows, own], local.at[0]).wait()
        for dy in (2, 1, 3):
            push(new_w.at[lower, own], new_w.at[lower, own], sa.at[5], ra.at[5], at(s, 0, dy, 0)).start()
        push(new_w.at[upper, own], new_w.at[upper, own], sa.at[3], ra.at[3], at(s, 0, 0, 1)).start()

    def gather_second():
        push(columns(1), columns(1), sa.at[3], ra.at[3], me).wait_recv()
        for dy in (2, 1, 3):
            push(new_w.at[upper, pair], new_w.at[upper, pair], sa.at[4], ra.at[4], at(s, 0, dy, 0)).start()
        push(columns(3), columns(3), sa.at[5], ra.at[5], me).wait_recv()
        for n in range(4):
            there = pl.ds(pl.multiple_of((n * 2 + h) * block, 128), block)
            push(new_w.at[lower, there], new_w.at[lower, there], sa.at[6], ra.at[6], at(s, 0, 0, 1)).start()

    def relay(i):
        data = jnp.dot(regroup[...], recv1[i].reshape(SLOTS, cols), preferred_element_type=jnp.float32)
        data = data.astype(jnp.bfloat16).reshape(4, 64, cols)
        send2[i] = data

        @pl.when((s == 1) | (s == 3))
        def _():
            for dy, dh in ((2, 0), (2, 1), (1, 0), (1, 1), (3, 0), (3, 1), (0, 1), (0, 0)):
                lines = pl.ds(dh * 32, 32)
                push(send2.at[i, dy, lines, :], arrived.at[i, dy, lines, :], s2.at[i], r2.at[i],
                     at(s - 1, 0, dy, dh)).start()

        @pl.when(s == 2)
        def _():
            middle[i, 0] = data[0]
            for dy in (2, 1, 3):
                push(send2.at[i, dy], middle.at[i, dy], s3.at[i], r3.at[i], at(2, 0, dy, 0)).start()

        @pl.when(s == 0)
        def _():
            for dy in (2, 1, 3, 0):
                push(send2.at[i, dy], arrived.at[i, dy], s2.at[i], r2.at[i], at(1, 0, dy, 0)).start()

    def three_rows(i):
        rows = pl.ds(1, 3)
        return push(send2.at[i, rows], middle.at[i, rows], s3.at[i], r3.at[i], at(2, 0, 1, 0))

    def forward(i):
        three_rows(i).wait_recv()
        for dh in (1, 0):
            lines = pl.ds(dh * 32, 32)
            push(middle.at[i, :, lines, :], arrived.at[i, :, lines, :], s2.at[i], r2.at[i], at(1, 0, 0, dh)).start()

    def squared(i):
        x = acts[:, span(i)].astype(jnp.float32)
        products_x = x * x
        total = squares[...]
        for c in range(cols // 128):
            total = total + products_x[:, c * 128:(c + 1) * 128]
        squares[...] = total

    def multiplied(i, g):
        terms = g * gain[:, span(i)] * acts[:, span(i)].astype(jnp.float32)
        total = products[...]
        for c in range(cols // 128):
            total = total + terms[:, c * 128:(c + 1) * 128]
        products[...] = total

    def keep(i):
        return pltpu.make_async_copy(grads.at[:, span(i)], grads_hbm.at[:, span(i)], out_sem.at[i])

    def take_loss(i):
        keep(i).start()
        multiplied(i, grads[:, span(i)].astype(jnp.float32))

    def take(i):
        whole(arrived, i, s2, r2).wait_recv()
        g = jnp.dot(natural[...], arrived[i].reshape(SLOTS, cols), preferred_element_type=jnp.float32)
        grads[:, span(i)] = g.astype(jnp.bfloat16)
        keep(i).start()
        multiplied(i, g)

    relays = lambda i: (s == 1) | (s == 3) | ((s == 2) & ~crossing(i)) | ((s == 0) & crossing(i))

    def step(i, carry):
        pl.when(i == 1)(lag_sum)
        pl.when(i == 3)(update)
        pl.when(i == 5)(gather_first)
        pl.when(i == 7)(gather_second)
        pl.when(relays(i))(lambda: along_z_all(i).wait_recv())
        pl.when((s == 0) & ~crossing(i) & (i + 3 < pieces))(lambda: onward(i + 3))
        pl.when(i + AHEAD < pieces)(lambda: (start_out(i + AHEAD, 0), None)[1])
        pl.when(relays(i))(lambda: relay(i))
        pl.when((s == 2) & crossing(i))(lambda: forward(i - 1))
        squared(i)
        pl.when(s == 3)(lambda: take_loss(i))
        pl.when((s < 3) & (i >= LAG))(lambda: take(i - LAG))
        return carry

    lax.fori_loop(0, pieces, step, 0)

    @pl.when(s < 3)
    def _():
        lax.fori_loop(pieces - LAG, pieces, lambda i, carry: (take(i), carry)[1], 0)

    def finish(i, carry):
        @pl.when(relays(i))
        def _():
            along_z_all(i).wait_send()
            whole(send2, i, s2, r2).wait_send()

        pl.when((s == 2) & ~crossing(i))(lambda: three_rows(i).wait_send())

        @pl.when((s == 2) & crossing(i))
        def _():
            whole(send2, i, s0, r0).wait_send()

        return carry

    lax.fori_loop(0, pieces, finish, 0)
    push(lag_in, lag_in, sa.at[0], ra.at[0], me).wait_send()
    push(part_in, part_in, sa.at[1], ra.at[1], me).wait_send()
    push(part_in, part_in, sa.at[2], ra.at[2], me).wait_send()
    push(columns(1), columns(1), sa.at[3], ra.at[3], me).wait_send()
    push(columns(3), columns(3), sa.at[5], ra.at[5], me).wait_send()
    push(columns(6), columns(6), sa.at[4], ra.at[4], me).wait()
    push(columns(4), columns(4), sa.at[6], ra.at[6], me).wait()
    lax.fori_loop(0, pieces, lambda i, carry: (keep(i).wait(), carry)[1], 0)


def norm(cols, gain_hbm, acts_hbm, grads_hbm, squares_hbm, products_hbm, fresh, out_hbm, new_w,
         gain, acts, grads, squares, products, out, held, small, acts_sem, grads_sem, out_sem):
    width = acts.shape[1]
    blocks = SLOTS // 32

    def lines(b):
        return pl.ds(pl.multiple_of(b * 32, 32), 32)

    def fetch_acts(b):
        return pltpu.make_async_copy(acts_hbm.at[lines(b), :], acts.at[lines(b), :], acts_sem.at[b])

    def fetch_grads(b):
        return pltpu.make_async_copy(grads_hbm.at[lines(b), :], grads.at[lines(b), :], grads_sem.at[b])

    def emit(b):
        return pltpu.make_async_copy(out.at[lines(b), :], out_hbm.at[lines(b), :], out_sem.at[b])

    firsts = [
        pltpu.make_async_copy(src, dst, small.at[n])
        for n, (src, dst) in enumerate(((gain_hbm, gain), (squares_hbm, squares), (products_hbm, products)))
    ]
    fetch_w = pltpu.make_async_copy(fresh, held, small.at[3])
    pass_on = pltpu.make_async_copy(held, new_w, small.at[4])
    for copy in firsts:
        copy.start()
    for b in range(blocks):
        fetch_acts(b).start()
        fetch_grads(b).start()
    fetch_w.start()
    for copy in firsts:
        copy.wait()

    def last(b, carry):
        fetch_acts(b).wait()
        fetch_grads(b).wait()
        for half in range(2):
            rows = pl.ds(pl.multiple_of(b * 32 + half * 16, 16), 16)
            r = lax.rsqrt(jnp.sum(squares[rows, :], axis=1, keepdims=True) / width + 1e-05)
            inner = jnp.sum(products[rows, :], axis=1, keepdims=True) * r / width
            for c in range(0, width, cols):
                at_cols = slice(c, c + cols)
                x = acts[rows, at_cols].astype(jnp.float32)
                g = grads[rows, at_cols].astype(jnp.float32)
                out[rows, at_cols] = (g + (g * gain[:, at_cols] - (x * r) * inner) * r).astype(jnp.bfloat16)
        emit(b).start()
        return carry

    lax.fori_loop(0, blocks // 2, last, 0)
    fetch_w.wait()
    pass_on.start()
    lax.fori_loop(blocks // 2, blocks, last, 0)
    lax.fori_loop(0, blocks, lambda b, carry: (emit(b).wait(), carry)[1], 0)
    pass_on.wait()


def per_device(send_grads, wiring, loss_grad, saved_acts, gain, lagged_grads, weights):
    rows, width = send_grads.shape
    pieces, cols = PIECES, width // PIECES
    depth = lagged_grads.shape[0]
    block = width // 8
    vmem = pl.BlockSpec(memory_space=pltpu.VMEM)
    hbm = pl.BlockSpec(memory_space=pl.ANY)
    bf16, f32 = jnp.bfloat16, jnp.float32
    dma = pltpu.SemaphoreType.DMA
    fresh, grads, squares, products = pl.pallas_call(
        functools.partial(exchange, pieces, cols),
        out_shape=(
            jax.ShapeDtypeStruct((depth, width), f32),
            jax.ShapeDtypeStruct((SLOTS, width), bf16),
            jax.ShapeDtypeStruct((SLOTS, 128), f32),
            jax.ShapeDtypeStruct((SLOTS, 128), f32),
        ),
        in_specs=[hbm] * 7,
        out_specs=(hbm, hbm, vmem, vmem),
        scratch_shapes=[
            pltpu.VMEM((pieces, 2, 128, cols), bf16),
            pltpu.VMEM((pieces, 2, 128, cols), bf16),
            pltpu.VMEM((pieces, 4, 64, cols), bf16),
            pltpu.VMEM((pieces, 4, 64, cols), bf16),
            pltpu.VMEM((pieces, 4, 64, cols), bf16),
            pltpu.VMEM((rows, width), bf16),
            pltpu.VMEM((SLOTS, width), bf16),
            pltpu.VMEM((SLOTS, width), bf16),
            pltpu.VMEM((1, rows), jnp.int32),
            pltpu.VMEM((1, width), f32),
            pltpu.VMEM((SLOTS, rows), bf16),
            pltpu.VMEM((SLOTS, SLOTS), bf16),
            pltpu.VMEM((SLOTS, SLOTS), bf16),
            pltpu.VMEM((depth, block), bf16),
            pltpu.VMEM((7, depth, block), bf16),
            pltpu.VMEM((depth, block), f32),
            pltpu.VMEM((7, 8, block), f32),
            pltpu.VMEM((8, block), f32),
            pltpu.VMEM((8, block), f32),
            dma((pieces,)), dma((pieces,)), dma((pieces,)), dma((pieces,)), dma((pieces,)), dma((pieces,)),
            dma((pieces,)), dma((pieces,)), dma((7,)), dma((7,)), dma((7,)), dma((pieces,)), dma((pieces,)),
        ],
        compiler_params=pltpu.CompilerParams(
            collective_id=0, has_side_effects=True, vmem_limit_bytes=59 * 1024 * 1024
        ),
        name="exchange",
    )(wiring.reshape(1, rows), gain, send_grads, lagged_grads, weights, loss_grad, saved_acts)
    return pl.pallas_call(
        functools.partial(norm, 512),
        out_shape=(
            jax.ShapeDtypeStruct((SLOTS, width), bf16),
            jax.ShapeDtypeStruct((depth, width), f32),
        ),
        in_specs=[hbm] * 6,
        out_specs=(hbm, hbm),
        scratch_shapes=[
            pltpu.VMEM((1, width), f32),
            pltpu.VMEM((SLOTS, width), bf16),
            pltpu.VMEM((SLOTS, width), bf16),
            pltpu.VMEM((SLOTS, 128), f32),
            pltpu.VMEM((SLOTS, 128), f32),
            pltpu.VMEM((SLOTS, width), bf16),
            pltpu.VMEM((depth, width), f32),
            dma((5,)), dma((SLOTS // 32,)), dma((SLOTS // 32,)), dma((SLOTS // 32,)),
        ],
        compiler_params=pltpu.CompilerParams(vmem_limit_bytes=59 * 1024 * 1024),
        name="norm",
    )(gain, saved_acts, grads, squares, products, fresh)


def solution(mesh):
    return jax.shard_map(
        per_device,
        mesh=mesh,
        in_specs=(
            P(("section", "peer"), None),
            P(("section", "peer"), None),
            P("peer", None),
            P(("section", "peer"), None),
            P("section", None),
            P("section", "peer"),
            P("section", None),
        ),
        out_specs=(P(("section", "peer"), None), P("section", None)),
        check_vma=False,
    )
```

```python
import functools

import jax
import jax.numpy as jnp
from jax import lax
from jax.experimental import pallas as pl
from jax.experimental.pallas import tpu as pltpu
from jax.sharding import PartitionSpec as P

MESH = pl.DeviceIdType.MESH
SLOTS = 256
CAP = 4
PIECES = 10
AHEAD = 3
LAG = 4


def place():
    s = lax.axis_index("section")
    p = lax.axis_index("peer")
    return s, p // 8, (p // 2) % 4, p % 2


def iota(shape, dim):
    return lax.broadcasted_iota(jnp.int32, shape, dim)


def slot_matrix(wire, z, y, h):
    rows = wire.shape[1]
    r, c = iota((rows, rows), 0), iota((rows, rows), 1)
    across = jnp.broadcast_to(wire, (rows, rows))
    down = jnp.sum(jnp.where(r == c, across, 0), axis=1, keepdims=True)
    rank = jnp.sum(jnp.where((down == across) & (r < c), 1, 0), axis=0, keepdims=True)
    key = wire * CAP + rank
    i = iota((SLOTS, rows), 0)
    dh, d, dy, k = i >> 7, (i >> 4) & 7, (i >> 2) & 3, i & 3
    q = ((z + d) & 7) * 8 + ((y + dy) & 3) * 2 + ((h + dh) & 1)
    return jnp.where(q * CAP + k == key, 1.0, 0.0).astype(jnp.bfloat16)


def regroup_matrix():
    o, i = iota((SLOTS, SLOTS), 0), iota((SLOTS, SLOTS), 1)
    dy, dh, d, k = o >> 6, (o >> 5) & 1, (o >> 2) & 7, o & 3
    return jnp.where(dh * 128 + d * 16 + dy * 4 + k == i, 1.0, 0.0).astype(jnp.bfloat16)


def natural_matrix(z, y, h):
    n, o = iota((SLOTS, SLOTS), 0), iota((SLOTS, SLOTS), 1)
    zs, ys, hs, k = n >> 5, (n >> 3) & 3, (n >> 2) & 1, n & 3
    d, dy, dh = (z - zs) & 7, (y - ys) & 3, (h - hs) & 1
    return jnp.where((dy * 2 + dh) * 32 + d * 4 + k == o, 1.0, 0.0).astype(jnp.bfloat16)


def exchange(pieces, cols, wire_hbm, gain_hbm, rows_hbm, lag_ref, w_ref, loss, acts_hbm, new_w, grads_hbm, squares, products,
             send1, recv1, send2, middle, arrived, rows_ref, acts, grads, wire, gain,
             slots, regroup, natural, lag_own, lag_in, part, part_in, fresh, w_own,
             s0, r0, s1, r1, s2, r2, s3, r3, sa, ra, local, row_sem, out_sem):
    s, z, y, h = place()
    width = lag_ref.shape[1]
    block = width // 8
    own = pl.ds(pl.multiple_of((y * 2 + h) * block, 128), block)
    zrows = pl.ds(pl.multiple_of(z * 8, 8), 8)

    def at(section, dz, dy, dh):
        peer = ((z + dz) % 8) * 8 + ((y + dy) % 4) * 2 + (h + dh) % 2
        return (section, peer)

    def push(src, dst, ssem, rsem, to):
        return pltpu.make_async_remote_copy(src_ref=src, dst_ref=dst, send_sem=ssem, recv_sem=rsem,
                                            device_id=to, device_id_type=MESH)

    me = at(s, 0, 0, 0)
    barrier = pltpu.get_barrier_semaphore()
    for d in range(1, 8):
        pl.semaphore_signal(barrier, inc=1, device_id=at(s, d, 0, 0), device_id_type=MESH)
    for e in range(8):
        for ds in range(4):
            if e or ds:
                pl.semaphore_signal(barrier, inc=1, device_id=at((s + ds) % 4, 0, e // 2, e % 2), device_id_type=MESH)

    crossing = lambda i: lax.rem(i, 2) == 1

    def span(i):
        return pl.ds(pl.multiple_of(i * cols, 128), cols)

    def fetch(i):
        return pltpu.make_async_copy(rows_hbm.at[:, span(i)], rows_ref.at[:, span(i)], row_sem.at[i])

    fetch_lag = pltpu.make_async_copy(lag_ref.at[:, own], lag_own, local.at[1])
    fetch_w = pltpu.make_async_copy(w_ref.at[zrows, own], w_own, local.at[2])
    fetch_acts = pltpu.make_async_copy(acts_hbm, acts, local.at[3])
    fetch_wire = pltpu.make_async_copy(wire_hbm, wire, local.at[5])
    fetch_gain = pltpu.make_async_copy(gain_hbm, gain, local.at[6])
    fetch_loss = pltpu.make_async_copy(loss, grads, local.at[4])

    fetch_wire.start()

    @pl.when(s >= 1)
    def _():
        for i in range(pieces):
            fetch(i).start()

    fetch_lag.start()
    fetch_gain.start()
    fetch_w.start()
    fetch_acts.start()
    pl.when(s == 3)(fetch_loss.start)
    squares[...] = jnp.zeros_like(squares)
    products[...] = jnp.zeros_like(products)

    fetch_wire.wait()
    slots[...] = slot_matrix(wire[...], z, y, h)

    def arrange(i):
        fetch(i).wait()
        data = jnp.dot(slots[...], rows_ref[:, span(i)], preferred_element_type=jnp.float32).astype(jnp.bfloat16)
        data = data.reshape(2, 128, cols)
        send1[i] = data
        recv1[i, :, 0:16, :] = data[:, 0:16, :]

    pl.when(s >= 1)(lambda: arrange(0))
    pl.semaphore_wait(barrier, 38)

    def lag_copy(e):
        dy, dh = e // 2, e % 2
        j = ((y + dy) % 4) * 2 + (h + dh) % 2
        return push(lag_ref.at[:, pl.ds(pl.multiple_of(j * block, 128), block)], lag_in.at[e - 1], sa.at[0], ra.at[0],
                    at(s, 0, dy, dh))

    for e in range(1, 8):
        lag_copy(e).start()

    def along_z(i, d):
        lines = pl.ds(d * 16, 16)
        return push(send1.at[i, :, lines, :], recv1.at[i, :, lines, :], s1.at[i], r1.at[i], at(s, d, 0, 0))

    def along_z_all(i):
        lines = pl.ds(16, 112)
        return push(send1.at[i, :, lines, :], recv1.at[i, :, lines, :], s1.at[i], r1.at[i], at(s, 1, 0, 0))

    def start_z(i):
        for d in (4, 3, 5, 2, 6, 1, 7):
            along_z(i, d).start()

    def cross(i, dh, first):
        lines = pl.ds(0, 16) if first else pl.ds(16, 112)
        return push(send1.at[i, dh, lines, :], (recv1 if first else send1).at[i, dh, lines, :],
                    s0.at[i], r0.at[i], at(0, 0, 0, dh))

    def whole(buffer, i, ssem, rsem):
        return push(buffer.at[i], buffer.at[i], ssem.at[i], rsem.at[i], at((s + 3) % 4, 0, 0, 0))

    def start_out(i, carry):
        @pl.when((s == 1) | (s == 3) | ((s == 2) & ~crossing(i)))
        def _():
            start_z(i)

        @pl.when((s == 2) & crossing(i))
        def _():
            for dh in range(2):
                cross(i, dh, False).start()
                cross(i, dh, True).start()

        return carry

    ahead = jnp.where(s == 2, AHEAD + 2, AHEAD)
    start_out(0, 0)

    @pl.when(s >= 1)
    def _():
        def arrange_start(i, carry):
            arrange(i)
            pl.when(i < ahead)(lambda: (start_out(i, 0), None)[1])
            return carry
        lax.fori_loop(1, pieces, arrange_start, 0)

    regroup[...] = regroup_matrix()
    natural[...] = natural_matrix(z, y, h)
    fetch_acts.wait()
    fetch_gain.wait()
    pl.when(s == 3)(fetch_loss.wait)

    def onward(i):
        whole(send2, i, s0, r0).wait_recv()
        start_z(i)

    @pl.when(s == 0)
    def _():
        onward(1)

    def lag_sum():
        push(lag_in, lag_in, sa.at[0], ra.at[0], me).wait_recv()
        fetch_lag.wait()
        total = lag_own[...].astype(jnp.float32)
        for e in range(7):
            total = total + lag_in[e].astype(jnp.float32)
        part[...] = total
        for d in range(1, 8):
            to = (z + d) % 8
            push(part.at[pl.ds(pl.multiple_of(to * 8, 8), 8)], part_in.at[d - 1], sa.at[1], ra.at[1],
                 at(s, d, 0, 0)).start()

    def update():
        push(part_in, part_in, sa.at[1], ra.at[1], me).wait_recv()
        total = part[zrows, :]
        for d in range(7):
            total = total + part_in[d]
        fetch_w.wait()
        fresh[...] = w_own[...] - 0.5 * (total / 64.0)
        for d in range(1, 8):
            push(fresh, new_w.at[zrows, own], sa.at[2], ra.at[2], at(s, d, 0, 0)).start()
        pltpu.make_async_copy(fresh, new_w.at[zrows, own], local.at[0]).start()

    half = new_w.shape[0] // 2
    upper, lower = pl.ds(0, half), pl.ds(half, half)
    pair = pl.ds(pl.multiple_of(y * 2 * block, 128), 2 * block)

    def columns(n):
        return new_w.at[upper, pl.ds(0, n * block)]

    def gather_first():
        push(part_in, part_in, sa.at[2], ra.at[2], me).wait_recv()
        pltpu.make_async_copy(fresh, new_w.at[zrows, own], local.at[0]).wait()
        for dy in (2, 1, 3):
            push(new_w.at[lower, own], new_w.at[lower, own], sa.at[5], ra.at[5], at(s, 0, dy, 0)).start()
        push(new_w.at[upper, own], new_w.at[upper, own], sa.at[3], ra.at[3], at(s, 0, 0, 1)).start()

    def gather_second():
        push(columns(1), columns(1), sa.at[3], ra.at[3], me).wait_recv()
        for dy in (2, 1, 3):
            push(new_w.at[upper, pair], new_w.at[upper, pair], sa.at[4], ra.at[4], at(s, 0, dy, 0)).start()
        push(columns(3), columns(3), sa.at[5], ra.at[5], me).wait_recv()
        for n in range(4):
            there = pl.ds(pl.multiple_of((n * 2 + h) * block, 128), block)
            push(new_w.at[lower, there], new_w.at[lower, there], sa.at[6], ra.at[6], at(s, 0, 0, 1)).start()

    def relay(i):
        data = jnp.dot(regroup[...], recv1[i].reshape(SLOTS, cols), preferred_element_type=jnp.float32)
        data = data.astype(jnp.bfloat16).reshape(4, 64, cols)
        send2[i] = data

        @pl.when((s == 1) | (s == 3))
        def _():
            for dy, dh in ((2, 0), (2, 1), (1, 0), (1, 1), (3, 0), (3, 1), (0, 1), (0, 0)):
                lines = pl.ds(dh * 32, 32)
                push(send2.at[i, dy, lines, :], arrived.at[i, dy, lines, :], s2.at[i], r2.at[i],
                     at(s - 1, 0, dy, dh)).start()

        @pl.when(s == 2)
        def _():
            middle[i, 0] = data[0]
            for dy in (2, 1, 3):
                push(send2.at[i, dy], middle.at[i, dy], s3.at[i], r3.at[i], at(2, 0, dy, 0)).start()

        @pl.when(s == 0)
        def _():
            for dy in (2, 1, 3, 0):
                push(send2.at[i, dy], arrived.at[i, dy], s2.at[i], r2.at[i], at(1, 0, dy, 0)).start()

    def three_rows(i):
        rows = pl.ds(1, 3)
        return push(send2.at[i, rows], middle.at[i, rows], s3.at[i], r3.at[i], at(2, 0, 1, 0))

    def forward(i):
        three_rows(i).wait_recv()
        for dh in (1, 0):
            lines = pl.ds(dh * 32, 32)
            push(middle.at[i, :, lines, :], arrived.at[i, :, lines, :], s2.at[i], r2.at[i], at(1, 0, 0, dh)).start()

    def squared(i):
        x = acts[:, span(i)].astype(jnp.float32)
        products_x = x * x
        total = squares[...]
        for c in range(cols // 128):
            total = total + products_x[:, c * 128:(c + 1) * 128]
        squares[...] = total

    def multiplied(i, g):
        terms = g * gain[:, span(i)] * acts[:, span(i)].astype(jnp.float32)
        total = products[...]
        for c in range(cols // 128):
            total = total + terms[:, c * 128:(c + 1) * 128]
        products[...] = total

    def keep(i):
        return pltpu.make_async_copy(grads.at[:, span(i)], grads_hbm.at[:, span(i)], out_sem.at[i])

    def take_loss(i):
        keep(i).start()
        multiplied(i, grads[:, span(i)].astype(jnp.float32))

    def take(i):
        whole(arrived, i, s2, r2).wait_recv()
        g = jnp.dot(natural[...], arrived[i].reshape(SLOTS, cols), preferred_element_type=jnp.float32)
        grads[:, span(i)] = g.astype(jnp.bfloat16)
        keep(i).start()
        multiplied(i, g)

    relays = lambda i: (s == 1) | (s == 3) | ((s == 2) & ~crossing(i)) | ((s == 0) & crossing(i))

    def step(i, carry):
        pl.when(i == 1)(lag_sum)
        pl.when(i == 3)(update)
        pl.when(i == 5)(gather_first)
        pl.when(i == 7)(gather_second)
        pl.when(relays(i))(lambda: along_z_all(i).wait_recv())
        pl.when((s == 0) & ~crossing(i) & (i + 3 < pieces))(lambda: onward(i + 3))
        pl.when(i + ahead < pieces)(lambda: (start_out(i + ahead, 0), None)[1])
        pl.when(relays(i))(lambda: relay(i))
        pl.when((s == 2) & crossing(i))(lambda: forward(i - 1))
        squared(i)
        pl.when(s == 3)(lambda: take_loss(i))
        pl.when((s < 3) & (i >= LAG))(lambda: take(i - LAG))
        return carry

    lax.fori_loop(0, pieces, step, 0)

    @pl.when(s < 3)
    def _():
        lax.fori_loop(pieces - LAG, pieces, lambda i, carry: (take(i), carry)[1], 0)

    def finish(i, carry):
        @pl.when(relays(i))
        def _():
            along_z_all(i).wait_send()
            whole(send2, i, s2, r2).wait_send()

        pl.when((s == 2) & ~crossing(i))(lambda: three_rows(i).wait_send())

        @pl.when((s == 2) & crossing(i))
        def _():
            whole(send2, i, s0, r0).wait_send()

        return carry

    lax.fori_loop(0, pieces, finish, 0)
    push(lag_in, lag_in, sa.at[0], ra.at[0], me).wait_send()
    push(part_in, part_in, sa.at[1], ra.at[1], me).wait_send()
    push(part_in, part_in, sa.at[2], ra.at[2], me).wait_send()
    push(columns(1), columns(1), sa.at[3], ra.at[3], me).wait_send()
    push(columns(3), columns(3), sa.at[5], ra.at[5], me).wait_send()
    push(columns(6), columns(6), sa.at[4], ra.at[4], me).wait()
    push(columns(4), columns(4), sa.at[6], ra.at[6], me).wait()
    lax.fori_loop(0, pieces, lambda i, carry: (keep(i).wait(), carry)[1], 0)


def norm(cols, gain_hbm, acts_hbm, grads_hbm, squares_hbm, products_hbm, fresh, out_hbm, new_w,
         gain, acts, grads, squares, products, out, held, small, acts_sem, grads_sem, out_sem):
    width = acts.shape[1]
    blocks = SLOTS // 32

    def lines(b):
        return pl.ds(pl.multiple_of(b * 32, 32), 32)

    def fetch_acts(b):
        return pltpu.make_async_copy(acts_hbm.at[lines(b), :], acts.at[lines(b), :], acts_sem.at[b])

    def fetch_grads(b):
        return pltpu.make_async_copy(grads_hbm.at[lines(b), :], grads.at[lines(b), :], grads_sem.at[b])

    def emit(b):
        return pltpu.make_async_copy(out.at[lines(b), :], out_hbm.at[lines(b), :], out_sem.at[b])

    firsts = [
        pltpu.make_async_copy(src, dst, small.at[n])
        for n, (src, dst) in enumerate(((gain_hbm, gain), (squares_hbm, squares), (products_hbm, products)))
    ]
    fetch_w = pltpu.make_async_copy(fresh, held, small.at[3])
    pass_on = pltpu.make_async_copy(held, new_w, small.at[4])
    for copy in firsts:
        copy.start()
    for b in range(blocks):
        fetch_acts(b).start()
        fetch_grads(b).start()
    fetch_w.start()
    for copy in firsts:
        copy.wait()

    def last(b, carry):
        fetch_acts(b).wait()
        fetch_grads(b).wait()
        for half in range(2):
            rows = pl.ds(pl.multiple_of(b * 32 + half * 16, 16), 16)
            r = lax.rsqrt(jnp.sum(squares[rows, :], axis=1, keepdims=True) / width + 1e-05)
            inner = jnp.sum(products[rows, :], axis=1, keepdims=True) * r / width
            for c in range(0, width, cols):
                at_cols = slice(c, c + cols)
                x = acts[rows, at_cols].astype(jnp.float32)
                g = grads[rows, at_cols].astype(jnp.float32)
                out[rows, at_cols] = (g + (g * gain[:, at_cols] - (x * r) * inner) * r).astype(jnp.bfloat16)
        emit(b).start()
        return carry

    lax.fori_loop(0, blocks // 2, last, 0)
    fetch_w.wait()
    pass_on.start()
    lax.fori_loop(blocks // 2, blocks, last, 0)
    lax.fori_loop(0, blocks, lambda b, carry: (emit(b).wait(), carry)[1], 0)
    pass_on.wait()


def per_device(send_grads, wiring, loss_grad, saved_acts, gain, lagged_grads, weights):
    rows, width = send_grads.shape
    pieces, cols = PIECES, width // PIECES
    depth = lagged_grads.shape[0]
    block = width // 8
    vmem = pl.BlockSpec(memory_space=pltpu.VMEM)
    hbm = pl.BlockSpec(memory_space=pl.ANY)
    bf16, f32 = jnp.bfloat16, jnp.float32
    dma = pltpu.SemaphoreType.DMA
    fresh, grads, squares, products = pl.pallas_call(
        functools.partial(exchange, pieces, cols),
        out_shape=(
            jax.ShapeDtypeStruct((depth, width), f32),
            jax.ShapeDtypeStruct((SLOTS, width), bf16),
            jax.ShapeDtypeStruct((SLOTS, 128), f32),
            jax.ShapeDtypeStruct((SLOTS, 128), f32),
        ),
        in_specs=[hbm] * 7,
        out_specs=(hbm, hbm, vmem, vmem),
        scratch_shapes=[
            pltpu.VMEM((pieces, 2, 128, cols), bf16),
            pltpu.VMEM((pieces, 2, 128, cols), bf16),
            pltpu.VMEM((pieces, 4, 64, cols), bf16),
            pltpu.VMEM((pieces, 4, 64, cols), bf16),
            pltpu.VMEM((pieces, 4, 64, cols), bf16),
            pltpu.VMEM((rows, width), bf16),
            pltpu.VMEM((SLOTS, width), bf16),
            pltpu.VMEM((SLOTS, width), bf16),
            pltpu.VMEM((1, rows), jnp.int32),
            pltpu.VMEM((1, width), f32),
            pltpu.VMEM((SLOTS, rows), bf16),
            pltpu.VMEM((SLOTS, SLOTS), bf16),
            pltpu.VMEM((SLOTS, SLOTS), bf16),
            pltpu.VMEM((depth, block), bf16),
            pltpu.VMEM((7, depth, block), bf16),
            pltpu.VMEM((depth, block), f32),
            pltpu.VMEM((7, 8, block), f32),
            pltpu.VMEM((8, block), f32),
            pltpu.VMEM((8, block), f32),
            dma((pieces,)), dma((pieces,)), dma((pieces,)), dma((pieces,)), dma((pieces,)), dma((pieces,)),
            dma((pieces,)), dma((pieces,)), dma((7,)), dma((7,)), dma((7,)), dma((pieces,)), dma((pieces,)),
        ],
        compiler_params=pltpu.CompilerParams(
            collective_id=0, has_side_effects=True, vmem_limit_bytes=59 * 1024 * 1024
        ),
        name="exchange",
    )(wiring.reshape(1, rows), gain, send_grads, lagged_grads, weights, loss_grad, saved_acts)
    return pl.pallas_call(
        functools.partial(norm, 512),
        out_shape=(
            jax.ShapeDtypeStruct((SLOTS, width), bf16),
            jax.ShapeDtypeStruct((depth, width), f32),
        ),
        in_specs=[hbm] * 6,
        out_specs=(hbm, hbm),
        scratch_shapes=[
            pltpu.VMEM((1, width), f32),
            pltpu.VMEM((SLOTS, width), bf16),
            pltpu.VMEM((SLOTS, width), bf16),
            pltpu.VMEM((SLOTS, 128), f32),
            pltpu.VMEM((SLOTS, 128), f32),
            pltpu.VMEM((SLOTS, width), bf16),
            pltpu.VMEM((depth, width), f32),
            dma((5,)), dma((SLOTS // 32,)), dma((SLOTS // 32,)), dma((SLOTS // 32,)),
        ],
        compiler_params=pltpu.CompilerParams(vmem_limit_bytes=59 * 1024 * 1024),
        name="norm",
    )(gain, saved_acts, grads, squares, products, fresh)


def solution(mesh):
    return jax.shard_map(
        per_device,
        mesh=mesh,
        in_specs=(
            P(("section", "peer"), None),
            P(("section", "peer"), None),
            P("peer", None),
            P(("section", "peer"), None),
            P("section", None),
            P("section", "peer"),
            P("section", None),
        ),
        out_specs=(P(("section", "peer"), None), P("section", None)),
        check_vma=False,
    )
```
